128 devices in a mesh: row: 16 (over z_hi, x, core), col: 8 (over z_lo, y).
Axes of the slice: x: 4, y: 4, z: 4 (z_hi: 2, z_lo: 2; z = z_hi * 2 + z_lo), core: 2. Of those that a mesh axis runs over, the one named last changes fastest.
Arguments:
- queries: bfloat16 [16384, 512], P(('row', 'col'))
- keys: bfloat16 [16384, 128], P(('row', 'col'))
- values: bfloat16 [16384, 128], P(('row', 'col')), may hold values from -6 to 6
- outputs: bfloat16 [16384, 512], P(('row', 'col')), may hold values from -6 to 6
- grad_out: bfloat16 [16384, 512], P(('row', 'col')), may hold values from -6 to 6
- block_order: int32 [128], replicated, may hold values from 0 to 127, each once
Outputs:
- grad_queries: bfloat16 [16384, 512], P(('row', 'col'))
- grad_keys: bfloat16 [16384, 128], P(('row', 'col'))
- grad_values: bfloat16 [16384, 128], P(('row', 'col'))
The draws below stay inside these ranges and needn't reach their ends.
Inputs may be any that keep to these rules, and one draw needn't show every extreme that they name: `block_order`: each slot holds a different block.
All inputs are finite; a program needn't handle non-finite values.
Results may differ from the reference program's by a relative error of at most 0.017.
Values may be sent and summed in bfloat16 or wider, within the bound.
A program may use at most 128 MiB of HBM per device.

```python
import math
import jax
import jax.numpy as jnp
from jax import lax

H = 4
DH = 128
BLK = 128
NB = 128
TOKENS = 16384


def shared_keys(key):
    return jax.random.normal(key, (TOKENS, DH), jnp.float32)


def draw_keys(key, part):
    base = shared_keys(key)
    return base.astype(jnp.bfloat16)


def draw_queries(key, part):
    key = jax.random.fold_in(key, 5)
    first = jax.random.fold_in(key, 0)
    result = jax.random.normal(first, (TOKENS, H * DH), jnp.float32)
    return result.astype(jnp.bfloat16)


def block_scale(stream_key, dims, pieces, low, top_value):
    level, own = 1.0, jax.random.fold_in(stream_key, 6)
    for dim, blocks in pieces:
        steps = jnp.exp(jax.random.uniform(jax.random.fold_in(own, dim), (blocks,), jnp.float32, low / len(pieces), top_value / len(pieces)))
        level = level * jnp.repeat(steps, dims[dim] // blocks).reshape([-1 if axis == dim else 1 for axis in range(len(dims))])
    return level


def bell_draw(stream_key, dims, scale, reach, pieces=(), kind=jnp.bfloat16):
    array = jax.random.normal(stream_key, dims, jnp.float32) * scale
    if len(pieces) > 0:
        array = block_scale(stream_key, dims, pieces, -0.22, 0.18) * array
    return jnp.clip(array, min=-reach, max=reach).astype(kind)


def setup_inputs(seed: int = 0) -> dict:
    arg_keys = jax.random.split(jax.random.key(seed), 7)
    queries = draw_queries(jax.random.fold_in(arg_keys[6], 71), 0)
    keys = draw_keys(jax.random.fold_in(arg_keys[6], 71), 0)
    values = bell_draw(arg_keys[2], (TOKENS, DH), 1.0, 6.0, ((0, 128),))
    outputs = bell_draw(arg_keys[3], (TOKENS, H * DH), 1.0, 6.0, ((0, 128),))
    grad_out = bell_draw(arg_keys[4], (TOKENS, H * DH), 1.0, 6.0, ((0, 128),))
    block_order = jax.random.permutation(arg_keys[5], NB).astype(jnp.int32)
    return {"queries": queries, "keys": keys, "values": values, "outputs": outputs, "grad_out": grad_out, "block_order": block_order}


def reference(queries, keys, values, outputs, grad_out, block_order):
    factor = 1.0 / math.sqrt(DH)
    positions = (block_order[:, None] * BLK + jnp.arange(BLK, dtype=jnp.int32)[None, :]).reshape(-1).astype(jnp.int32)
    q_rows = 512 if TOKENS % 512 == 0 else TOKENS
    count = TOKENS // q_rows
    key_float = keys.astype(jnp.float32)
    value_float = values.astype(jnp.float32)

    def step(carry, number):
        grad_k, grad_v = carry
        offset = (number * q_rows).astype(jnp.int32)
        query_block = lax.dynamic_slice_in_dim(queries, offset, q_rows, 0).astype(jnp.float32).reshape(q_rows, H, DH)
        out_block = lax.dynamic_slice_in_dim(outputs, offset, q_rows, 0).astype(jnp.float32).reshape(q_rows, H, DH)
        cot_block = lax.dynamic_slice_in_dim(grad_out, offset, q_rows, 0).astype(jnp.float32).reshape(q_rows, H, DH)
        query_pos = lax.dynamic_slice_in_dim(positions, offset, q_rows, 0)
        causal = positions[None, :] <= query_pos[:, None]
        scores = jnp.einsum('qhd,kd->hqk', query_block, key_float) * factor
        scores = jnp.where(causal[None], scores, -1e+30)
        largest = lax.optimization_barrier(jnp.max(scores, axis=-1, keepdims=True))
        total = lax.optimization_barrier(jnp.sum(jnp.where(causal[None], jnp.exp(scores - largest), 0.0), axis=-1, keepdims=True))
        log_total = largest + jnp.log(total)
        probs = jnp.where(causal[None], jnp.exp(scores - log_total), 0.0)
        probs_half = lax.optimization_barrier(probs.astype(jnp.bfloat16)).astype(jnp.float32)
        delta = jnp.transpose(lax.optimization_barrier(jnp.sum(cot_block * out_block, axis=-1)))
        grad_p = jnp.einsum('qhd,kd->hqk', cot_block, value_float)
        grad_s = probs * (grad_p - delta[:, :, None]) * factor
        grad_s = lax.optimization_barrier(grad_s.astype(jnp.bfloat16)).astype(jnp.float32)
        grad_q = jnp.einsum('hqk,kd->qhd', grad_s, key_float).reshape(q_rows, H * DH).astype(jnp.bfloat16)
        grad_k = grad_k + jnp.einsum('hqk,qhd->kd', grad_s, query_block)
        grad_v = grad_v + jnp.einsum('hqk,qhd->kd', probs_half, cot_block)
        return ((grad_k, grad_v), grad_q)
    zeros = jnp.zeros((TOKENS, DH), jnp.float32)
    (grad_k, grad_v), grad_q = lax.scan(step, (zeros, zeros), jnp.arange(count, dtype=jnp.int32))
    return (grad_q.reshape(TOKENS, H * DH), grad_k.astype(jnp.bfloat16), grad_v.astype(jnp.bfloat16))
```

```python
import functools
import math

import jax
import jax.numpy as jnp
from jax import lax
from jax.experimental import pallas as pl
from jax.experimental.pallas import tpu as pltpu
from jax.sharding import PartitionSpec as P

MESH = pl.DeviceIdType.MESH
F32 = jnp.float32
BF16 = jnp.bfloat16
HIDDEN = -1e30

NQ = 8
NK = 16


def here():
    row = lax.axis_index("row")
    col = lax.axis_index("col")
    z = (row // 8) * 2 + col // 4
    return (row // 2) % 4, col % 4, z, row % 2


def device(x, y, z, core):
    return (((z // 2) * 4 + x) * 2 + core, (z % 2) * 4 + y)


def y_step(t):
    u = t // 2
    return u + (u // 2) * (5 - 2 * u)


def query_owner(t):
    x, y, z, core = here()
    return x, (y + 4 - y_step(t)) % 4, z, (core + t % 2) % 2


def query_reader(t):
    x, y, z, core = here()
    return x, (y + y_step(t)) % 4, z, (core + t % 2) % 2


def key_owner(j):
    x, y, z, core = here()
    return (x + 4 - j % 4) % 4, y, (z + 4 - j // 4) % 4, core


def key_reader(j):
    x, y, z, core = here()
    return (x + j % 4) % 4, y, (z + j // 4) % 4, core


def slot_of(place):
    row, col = device(*place)
    return row * 8 + col


def kernel(
    order,
    q_in,
    k_in,
    v_in,
    o_in,
    g_in,
    dq_out,
    dk_out,
    dv_out,
    qs,
    gs,
    own_o,
    delta,
    ks,
    vs,
    kt,
    scores,
    probs,
    dscores,
    u_mine,
    u_got,
    stat,
    stat_got,
    cmat,
    qc,
    gc,
    part,
    part_got,
    local_sem,
    q_send,
    q_recv,
    d_send,
    d_recv,
    k_send,
    k_recv,
    u_send,
    u_recv,
    s_send,
    s_recv,
    p_send,
    p_recv,
):
    dh = 128
    blk = 128
    heads = 4
    factor = 1.0 / math.sqrt(dh)
    scale2 = factor * math.log2(math.e)

    def remote(src, dst, send, recv, place):
        return pltpu.make_async_remote_copy(
            src_ref=src,
            dst_ref=dst,
            send_sem=send,
            recv_sem=recv,
            device_id=device(*place),
            device_id_type=MESH,
        )

    def q_copy(src_q, src_g, t, place):
        return (
            remote(src_q, qs.at[t], q_send.at[t, 0], q_recv.at[t, 0], place),
            remote(src_g, gs.at[t], q_send.at[t, 1], q_recv.at[t, 1], place),
        )

    def k_copy(j):
        rows = pl.ds(j * blk, blk)
        return (
            remote(k_in, ks.at[rows], k_send.at[j, 0], k_recv.at[j, 0], key_reader(j)),
            remote(v_in, vs.at[rows], k_send.at[j, 1], k_recv.at[j, 1], key_reader(j)),
        )

    def d_copy(t):
        return remote(delta.at[0], delta.at[t], d_send.at[t], d_recv.at[t], query_reader(t))

    def u_copy(t):
        return remote(u_mine.at[t], u_got.at[t], u_send.at[t], u_recv.at[t], query_owner(t))

    def s_copy(t):
        return remote(stat, stat_got.at[t], s_send.at[t], s_recv.at[t], query_owner(t))

    def p_copy(j):
        return remote(part.at[j], part_got.at[j], p_send.at[j], p_recv.at[j], key_owner(j))

    barrier = pltpu.get_barrier_semaphore()
    for t in range(1, NQ):
        pl.semaphore_signal(barrier, inc=1, device_id=device(*query_reader(t)), device_id_type=MESH)
    for j in range(1, NK):
        pl.semaphore_signal(barrier, inc=1, device_id=device(*key_reader(j)), device_id_type=MESH)
    locals_ = [
        pltpu.make_async_copy(o_in, own_o, local_sem.at[0]),
        pltpu.make_async_copy(g_in, gs.at[0], local_sem.at[1]),
        pltpu.make_async_copy(q_in, qs.at[0], local_sem.at[2]),
        pltpu.make_async_copy(k_in, ks.at[pl.ds(0, blk)], local_sem.at[3]),
        pltpu.make_async_copy(v_in, vs.at[pl.ds(0, blk)], local_sem.at[4]),
    ]
    for copy in locals_:
        copy.start()
    for copy in locals_:
        copy.wait()
    product = gs[0].astype(F32) * own_o[...].astype(F32)
    for h in range(heads):
        summed = jnp.sum(product[:, h * dh : (h + 1) * dh], axis=1, keepdims=True)
        wide = jnp.broadcast_to(summed, (blk, dh))
        delta[0, :, h * blk : (h + 1) * blk] = jnp.transpose(wide)[0:1, :]
    pl.semaphore_wait(barrier, NQ - 1 + NK - 1)

    for j in range(1, NK):
        for copy in k_copy(j):
            copy.start()
    for t in (1, 2, 4, 6):
        for copy in q_copy(q_in, g_in, t, query_reader(t)):
            copy.start()
    for t in range(1, NQ):
        d_copy(t).start()

    for j in range(1, NK):
        for copy in k_copy(j):
            copy.wait_recv()
    for j in range(NK):
        kt[:, j * blk : (j + 1) * blk] = jnp.transpose(
            ks[j * blk : (j + 1) * blk, :].astype(F32)
        ).astype(BF16)

    x, y, z, core = here()
    row_less_col = lax.broadcasted_iota(jnp.int32, (blk, 2 * blk), 0) - (
        lax.broadcasted_iota(jnp.int32, (blk, 2 * blk), 1) % blk
    )
    chunk = 256
    per_chunk = chunk // blk

    def step(t, carry):
        @pl.when(t > 0)
        def _():
            for copy in q_copy(q_in, g_in, t, query_reader(t)):
                copy.wait_recv()
            d_copy(t).wait_recv()

        @pl.when(jnp.logical_and(t > 1, t % 2 == 0))
        def _():
            for copy in q_copy(qs.at[t], gs.at[t], t + 1, (x, y, z, (core + 1) % 2)):
                copy.start()

        owner = query_owner(t)
        q_order = order[slot_of(owner)]
        group = owner[1] * 2 + owner[3]
        for pair in range(2):
            lanes = pl.ds(pl.multiple_of(t * 512 + pair * 256, 256), 256)
            own = slice(pair * 256, pair * 256 + 256)
            q2 = jnp.concatenate(
                [qs[t, :, (2 * pair + i) * dh : (2 * pair + i + 1) * dh] for i in range(2)], axis=0
            )
            g2 = jnp.concatenate(
                [gs[t, :, (2 * pair + i) * dh : (2 * pair + i + 1) * dh] for i in range(2)], axis=0
            )
            top8 = jnp.full((8, 256), HIDDEN, F32)
            penalty = []
            for first in range(0, NK, per_chunk):
                rows = slice(first * blk, (first + per_chunk) * blk)
                s = lax.dot_general(
                    ks[rows, :], q2, (((1,), (1,)), ((), ())), preferred_element_type=F32
                )
                for i in range(per_chunk):
                    j = first + i
                    tile = s[i * blk : (i + 1) * blk]
                    k_order = order[slot_of(key_owner(j))]
                    if j == 0:
                        tile = jnp.where(row_less_col <= blk * (q_order - k_order), tile, HIDDEN)
                        cost = jnp.float32(0.0)
                    else:
                        cost = jnp.where(k_order < q_order, 0.0, -HIDDEN).astype(F32)
                    penalty.append(cost)
                    scores[j * blk : (j + 1) * blk, :] = tile
                    largest = jnp.max(tile.reshape(blk // 8, 8, 256), axis=0)
                    top8 = jnp.maximum(top8, largest - cost)
            top = jnp.max(top8, axis=0, keepdims=True) * scale2
            total8 = jnp.zeros((8, 256), F32)
            du = jnp.zeros((dh, 256), F32)
            away = delta[t, :, own]
            for first in range(0, NK, per_chunk):
                rows = slice(first * blk, (first + per_chunk) * blk)
                dp = lax.dot_general(
                    vs[rows, :], g2, (((1,), (1,)), ((), ())), preferred_element_type=F32
                )
                pieces = []
                for i in range(per_chunk):
                    j = first + i
                    tile_rows = slice(j * blk, (j + 1) * blk)
                    p = jnp.exp2(scores[tile_rows, :] * scale2 - (top + penalty[j]))
                    total8 += jnp.sum(p.reshape(blk // 8, 8, 256), axis=0)
                    ds = (p * (dp[i * blk : (i + 1) * blk] - away)).astype(BF16)
                    probs[tile_rows, lanes] = p.astype(BF16)
                    dscores[tile_rows, lanes] = ds
                    pieces.append(ds)
                du += jnp.dot(
                    kt[:, rows], jnp.concatenate(pieces, axis=0), preferred_element_type=F32
                )
            u_mine[t, :, own] = du.astype(BF16)
            stat[0, pl.ds(group, 1), own] = top
            stat[1, pl.ds(group, 1), own] = jnp.sum(total8, axis=0, keepdims=True)

        @pl.when(t > 0)
        def _():
            u_copy(t).start()

        return carry

    lax.fori_loop(0, NQ, step, 0)

    for t in range(1, NQ):
        s_copy(t).start()
    for t in range(1, NQ):
        s_copy(t).wait_recv()
    tops = [stat[0]] + [stat_got[t, 0] for t in range(1, NQ)]
    best = functools.reduce(jnp.maximum, tops)
    total = stat[1] * jnp.exp2(tops[0] - best)
    for t in range(1, NQ):
        total += stat_got[t, 1] * jnp.exp2(tops[t] - best)
    log_total = best + jnp.log2(total)
    cmat[0] = jnp.exp2(stat[0] - log_total)
    for t in range(1, NQ):
        cmat[t] = jnp.exp2(stat_got[t, 0] - log_total)

    def line_of(matrix, place):
        line = lax.broadcasted_iota(jnp.int32, matrix.shape, 0)
        picked = jnp.where(line == place[1] * 2 + place[3], matrix, 0.0)
        return jnp.sum(picked, axis=0, keepdims=True)

    rows = []
    for t in range(NQ):
        line = line_of(cmat[0], query_owner(t))
        for h in range(heads):
            rows.append(line[:, h * blk : (h + 1) * blk])
    rows.append(jnp.zeros((blk - NQ * heads, blk), F32))
    columns = jnp.transpose(jnp.concatenate(rows, axis=0))
    for t in range(NQ):
        for h in range(heads):
            place = slice((t * heads + h) * blk, (t * heads + h + 1) * blk)
            c = columns[:, t * heads + h : t * heads + h + 1]
            qc[place, :] = (qs[t, :, h * dh : (h + 1) * dh].astype(F32) * c).astype(BF16)
            gc[place, :] = (gs[t, :, h * dh : (h + 1) * dh].astype(F32) * c).astype(BF16)

    def grads(i, carry):
        dz = 3 - i
        rows = pl.ds(pl.multiple_of(dz * 512, 512), 512)
        dv = jnp.dot(probs[rows, :], gc[...], preferred_element_type=F32)
        dk = jnp.dot(dscores[rows, :], qc[...], preferred_element_type=F32) * factor
        for n in range(4):
            j = dz * 4 + n
            part[j, 0] = dk[n * blk : (n + 1) * blk].astype(BF16)
            part[j, 1] = dv[n * blk : (n + 1) * blk].astype(BF16)

            @pl.when(j > 0)
            def _():
                p_copy(j).start()

        return carry

    lax.fori_loop(0, 4, grads, 0)

    for t in range(1, NQ):
        u_copy(t).wait_recv()
    weights = [line_of(cmat[t], (x, y, z, core)) * factor for t in range(NQ)]
    for h in range(heads):
        lanes = slice(h * blk, (h + 1) * blk)
        acc = weights[0][:, lanes] * u_mine[0, :, lanes].astype(F32)
        for t in range(1, NQ):
            acc += weights[t][:, lanes] * u_got[t, :, lanes].astype(F32)
        dq_out[:, h * dh : (h + 1) * dh] = jnp.transpose(acc).astype(BF16)

    for j in range(1, NK):
        p_copy(j).wait_recv()
    dk_sum = part[0, 0].astype(F32)
    dv_sum = part[0, 1].astype(F32)
    for j in range(1, NK):
        dk_sum += part_got[j, 0].astype(F32)
        dv_sum += part_got[j, 1].astype(F32)
    dk_out[...] = dk_sum.astype(BF16)
    dv_out[...] = dv_sum.astype(BF16)

    for j in range(1, NK):
        for copy in k_copy(j):
            copy.wait_send()
        p_copy(j).wait_send()
    for t in range(1, NQ):
        for copy in q_copy(q_in, g_in, t, query_reader(t)):
            copy.wait_send()
        d_copy(t).wait_send()
        u_copy(t).wait_send()
        s_copy(t).wait_send()


def per_device(queries, keys, values, outputs, grad_out, block_order):
    anywhere = pl.BlockSpec(memory_space=pl.ANY)
    whole = pl.BlockSpec(memory_space=pltpu.VMEM)
    dma = pltpu.SemaphoreType.DMA
    return pl.pallas_call(
        kernel,
        out_shape=(
            jax.ShapeDtypeStruct((128, 512), BF16),
            jax.ShapeDtypeStruct((128, 128), BF16),
            jax.ShapeDtypeStruct((128, 128), BF16),
        ),
        in_specs=[pl.BlockSpec(memory_space=pltpu.SMEM)] + [anywhere] * 5,
        out_specs=(whole, whole, whole),
        scratch_shapes=[
            pltpu.VMEM((NQ, 128, 512), BF16),
            pltpu.VMEM((NQ, 128, 512), BF16),
            pltpu.VMEM((128, 512), BF16),
            pltpu.VMEM((NQ, 1, 512), F32),
            pltpu.VMEM((2048, 128), BF16),
            pltpu.VMEM((2048, 128), BF16),
            pltpu.VMEM((128, 2048), BF16),
            pltpu.VMEM((2048, 256), F32),
            pltpu.VMEM((2048, 4096), BF16),
            pltpu.VMEM((2048, 4096), BF16),
            pltpu.VMEM((NQ, 128, 512), BF16),
            pltpu.VMEM((NQ, 128, 512), BF16),
            pltpu.VMEM((2, NQ, 512), F32),
            pltpu.VMEM((NQ, 2, NQ, 512), F32),
            pltpu.VMEM((NQ, NQ, 512), F32),
            pltpu.VMEM((4096, 128), BF16),
            pltpu.VMEM((4096, 128), BF16),
            pltpu.VMEM((NK, 2, 128, 128), BF16),
            pltpu.VMEM((NK, 2, 128, 128), BF16),
            dma((5,)),
            dma((NQ, 2)),
            dma((NQ, 2)),
            dma((NQ,)),
            dma((NQ,)),
            dma((NK, 2)),
            dma((NK, 2)),
            dma((NQ,)),
            dma((NQ,)),
            dma((NQ,)),
            dma((NQ,)),
            dma((NK,)),
            dma((NK,)),
        ],
        compiler_params=pltpu.CompilerParams(
            collective_id=0, has_side_effects=True, vmem_limit_bytes=60 * 1024 * 1024
        ),
        name="attention_backward",
    )(block_order, queries, keys, values, outputs, grad_out)


def solution(mesh):
    rows = P(("row", "col"), None)
    return jax.shard_map(
        per_device,
        mesh=mesh,
        in_specs=(rows, rows, rows, rows, rows, P()),
        out_specs=(rows, rows, rows),
        check_vma=False,
    )
```

```python
import functools
import math

import jax
import jax.numpy as jnp
from jax import lax
from jax.experimental import pallas as pl
from jax.experimental.pallas import tpu as pltpu
from jax.sharding import PartitionSpec as P

MESH = pl.DeviceIdType.MESH
F32 = jnp.float32
BF16 = jnp.bfloat16
HIDDEN = -1e30

NQ = 8
NK = 16
KEY_STEPS = (
    ((0, 0), (1, 0), (3, 0), (0, 1), (0, 3), (1, 1), (3, 3), (1, 3))
    + ((2, 2), (2, 1), (2, 3), (1, 2), (3, 2), (2, 0), (0, 2), (3, 1))
)
FAR_ORDER = (13, 14, 15, 9, 10, 11, 12, 8)
HALF = 1024


def here():
    row = lax.axis_index("row")
    col = lax.axis_index("col")
    z = (row // 8) * 2 + col // 4
    return (row // 2) % 4, col % 4, z, row % 2


def device(x, y, z, core):
    return (((z // 2) * 4 + x) * 2 + core, (z % 2) * 4 + y)


def y_step(t):
    u = t // 2
    return u + (u // 2) * (5 - 2 * u)


def query_owner(t):
    x, y, z, core = here()
    return x, (y + 4 - y_step(t)) % 4, z, (core + t % 2) % 2


def query_reader(t):
    x, y, z, core = here()
    return x, (y + y_step(t)) % 4, z, (core + t % 2) % 2


def key_owner(j):
    x, y, z, core = here()
    dx, dz = KEY_STEPS[j]
    return (x + 4 - dx) % 4, y, (z + 4 - dz) % 4, core


def key_reader(j):
    x, y, z, core = here()
    dx, dz = KEY_STEPS[j]
    return (x + dx) % 4, y, (z + dz) % 4, core


def static_y(t):
    return (0, 1, 3, 2)[t // 2]


def seen_as(sender, t):
    dy = (static_y(t) - static_y(sender)) % 4
    return 2 * (0, 1, 3, 2)[dy] + (sender + t) % 2


def slot_of(place):
    row, col = device(*place)
    return row * 8 + col


def kernel(
    order,
    q_in,
    k_in,
    v_in,
    o_in,
    g_in,
    dq_out,
    dk_out,
    dv_out,
    qs,
    gs,
    own_o,
    delta,
    ks,
    vs,
    kt,
    scores,
    probs,
    dscores,
    u_sum,
    u_mine,
    u_got,
    stat_first,
    stat,
    stat_got,
    columns,
    qc,
    gc,
    part,
    part_got,
    local_sem,
    q_send,
    q_recv,
    d_send,
    d_recv,
    k_send,
    k_recv,
    u_send,
    u_recv,
    s_send,
    s_recv,
    p_send,
    p_recv,
):
    dh = 128
    blk = 128
    heads = 4
    factor = 1.0 / math.sqrt(dh)
    scale2 = factor * math.log2(math.e)

    def remote(src, dst, send, recv, place):
        return pltpu.make_async_remote_copy(
            src_ref=src,
            dst_ref=dst,
            send_sem=send,
            recv_sem=recv,
            device_id=device(*place),
            device_id_type=MESH,
        )

    def q_copy(src_q, src_g, t, place):
        return (
            remote(src_q, qs.at[t], q_send.at[t, 0], q_recv.at[t, 0], place),
            remote(src_g, gs.at[t], q_send.at[t, 1], q_recv.at[t, 1], place),
        )

    def k_copy(j):
        rows = pl.ds(j * blk, blk)
        return (
            remote(k_in, ks.at[rows], k_send.at[j, 0], k_recv.at[j, 0], key_reader(j)),
            remote(v_in, vs.at[rows], k_send.at[j, 1], k_recv.at[j, 1], key_reader(j)),
        )

    def d_copy(t):
        return remote(delta.at[0], delta.at[t], d_send.at[t], d_recv.at[t], query_reader(t))

    def u_copy(t):
        return remote(u_mine.at[t], u_got.at[t], u_send.at[t], u_recv.at[t], query_owner(t))

    def s_copy(t, batch):
        some = pl.ds(batch * 4, 4)
        return remote(
            stat.at[some],
            stat_got.at[t, some],
            s_send.at[t, batch],
            s_recv.at[t, batch],
            query_owner(t),
        )

    def p_copy(j):
        return remote(part.at[j], part_got.at[j], p_send.at[j], p_recv.at[j], key_owner(j))

    barrier = pltpu.get_barrier_semaphore()
    for t in range(1, NQ):
        pl.semaphore_signal(barrier, inc=1, device_id=device(*query_reader(t)), device_id_type=MESH)
    for j in range(1, NK):
        pl.semaphore_signal(barrier, inc=1, device_id=device(*key_reader(j)), device_id_type=MESH)
    locals_ = [
        pltpu.make_async_copy(o_in, own_o, local_sem.at[0]),
        pltpu.make_async_copy(g_in, gs.at[0], local_sem.at[1]),
        pltpu.make_async_copy(q_in, qs.at[0], local_sem.at[2]),
        pltpu.make_async_copy(k_in, ks.at[pl.ds(0, blk)], local_sem.at[3]),
        pltpu.make_async_copy(v_in, vs.at[pl.ds(0, blk)], local_sem.at[4]),
    ]
    for copy in locals_:
        copy.start()
    for copy in locals_:
        copy.wait()
    product = gs[0].astype(F32) * own_o[...].astype(F32)
    for h in range(heads):
        summed = jnp.sum(product[:, h * dh : (h + 1) * dh], axis=1, keepdims=True)
        wide = jnp.broadcast_to(summed, (blk, dh))
        delta[0, :, h * blk : (h + 1) * blk] = jnp.transpose(wide)[0:1, :]
    pl.semaphore_wait(barrier, NQ - 1 + NK - 1)

    def start_keys(slots):
        for j in slots:
            for copy in k_copy(j):
                copy.start()

    start_keys(range(1, 5))
    for t in (1, 2, 4):
        for copy in q_copy(q_in, g_in, t, query_reader(t)):
            copy.start()
    start_keys(range(5, 8))
    for t in range(1, NQ):
        d_copy(t).start()
    start_keys(FAR_ORDER)
    for copy in q_copy(q_in, g_in, 6, query_reader(6)):
        copy.start()

    def take_keys(slots):
        for j in slots:
            if j > 0:
                for copy in k_copy(j):
                    copy.wait_recv()
        for j in slots:
            kt[:, j * blk : (j + 1) * blk] = jnp.transpose(
                ks[j * blk : (j + 1) * blk, :].astype(F32)
            ).astype(BF16)

    x, y, z, core = here()
    row_less_col = lax.broadcasted_iota(jnp.int32, (blk, 2 * blk), 0) - (
        lax.broadcasted_iota(jnp.int32, (blk, 2 * blk), 1) % blk
    )
    chunk = 256
    per_chunk = chunk // blk

    def unit(t, half, with_u):
        q_order = order[slot_of(query_owner(t))]
        slots = range(half * 8, half * 8 + 8)
        for pair in range(2):
            lanes = pl.ds(pl.multiple_of(t * 512 + pair * 256, 256), 256)
            own = slice(pair * 256, pair * 256 + 256)
            q2 = jnp.concatenate(
                [qs[t, :, (2 * pair + i) * dh : (2 * pair + i + 1) * dh] for i in range(2)], axis=0
            )
            g2 = jnp.concatenate(
                [gs[t, :, (2 * pair + i) * dh : (2 * pair + i + 1) * dh] for i in range(2)], axis=0
            )
            top8 = jnp.full((8, 256), HIDDEN, F32)
            penalty = {}
            for first in slots[::per_chunk]:
                rows = slice(first * blk, (first + per_chunk) * blk)
                s = lax.dot_general(
                    ks[rows, :], q2, (((1,), (1,)), ((), ())), preferred_element_type=F32
                )
                for i in range(per_chunk):
                    j = first + i
                    n = j - half * 8
                    tile = s[i * blk : (i + 1) * blk]
                    k_order = order[slot_of(key_owner(j))]
                    if j == 0:
                        tile = jnp.where(row_less_col <= blk * (q_order - k_order), tile, HIDDEN)
                        cost = jnp.float32(0.0)
                    else:
                        cost = jnp.where(k_order < q_order, 0.0, -HIDDEN).astype(F32)
                    penalty[j] = cost
                    scores[n * blk : (n + 1) * blk, :] = tile
                    largest = jnp.max(tile.reshape(blk // 8, 8, 256), axis=0)
                    top8 = jnp.maximum(top8, largest - cost)
            top = jnp.max(top8, axis=0, keepdims=True) * scale2
            if half == 1:
                before = stat_first[t, 0:1, own]
                top = jnp.maximum(top, before)
            total8 = jnp.zeros((8, 256), F32)
            du = jnp.zeros((dh, 256), F32)
            away = delta[t, :, own]
            for first in slots[::per_chunk]:
                rows = slice(first * blk, (first + per_chunk) * blk)
                dp = lax.dot_general(
                    vs[rows, :], g2, (((1,), (1,)), ((), ())), preferred_element_type=F32
                )
                pieces = []
                for i in range(per_chunk):
                    j = first + i
                    n = j - half * 8
                    tile_rows = slice(j * blk, (j + 1) * blk)
                    p = jnp.exp2(
                        scores[n * blk : (n + 1) * blk, :] * scale2 - (top + penalty[j])
                    )
                    total8 += jnp.sum(p.reshape(blk // 8, 8, 256), axis=0)
                    ds = (p * (dp[i * blk : (i + 1) * blk] - away)).astype(BF16)
                    probs[tile_rows, lanes] = p.astype(BF16)
                    dscores[tile_rows, lanes] = ds
                    pieces.append(ds)
                if with_u:
                    du += jnp.dot(
                        kt[:, rows], jnp.concatenate(pieces, axis=0), preferred_element_type=F32
                    )
            total = jnp.sum(total8, axis=0, keepdims=True)
            if half == 0:
                stat_first[t, 0:1, own] = top
                stat_first[t, 1:2, own] = total
                u_sum[t, :, own] = du
            else:
                shrink = jnp.exp2(before - top)
                stat[t, 0:1, own] = top
                stat[t, 1:2, own] = total + stat_first[t, 1:2, own] * shrink
                if with_u:
                    u_mine[t, :, own] = (du + u_sum[t, :, own] * shrink).astype(BF16)

    def first_half(t, carry):
        @pl.when(t > 0)
        def _():
            for copy in q_copy(q_in, g_in, t, query_reader(t)):
                copy.wait_recv()
            d_copy(t).wait_recv()

        @pl.when(jnp.logical_and(t > 1, t % 2 == 0))
        def _():
            for copy in q_copy(qs.at[t], gs.at[t], t + 1, (x, y, z, (core + 1) % 2)):
                copy.start()

        unit(t, 0, True)
        return carry

    def second_half(t, carry):
        unit(t, 1, True)

        @pl.when(t > 0)
        def _():
            u_copy(t).start()

        return carry

    def second_half_late(t, carry):
        unit(t, 1, False)
        return carry

    def late_u(t, carry):
        lanes = pl.ds(pl.multiple_of(t * 512, 512), 512)
        du = jnp.dot(kt[:, HALF:], dscores[HALF:, lanes], preferred_element_type=F32)
        shrink = jnp.exp2(stat_first[t, 0:1, :] - stat[t, 0:1, :])
        u_mine[t] = (du + u_sum[t] * shrink).astype(BF16)
        u_copy(t).start()
        return carry

    take_keys(range(8))
    lax.fori_loop(0, NQ, first_half, 0)
    take_keys(range(8, NK))
    lax.fori_loop(0, 4, second_half, 0)
    for t in range(1, NQ):
        s_copy(t, 0).start()
    lax.fori_loop(4, NQ, second_half_late, 0)
    for t in range(1, NQ):
        s_copy(t, 1).start()
    lax.fori_loop(4, NQ, late_u, 0)

    for t in range(1, NQ):
        for batch in range(2):
            s_copy(t, batch).wait_recv()
    found = {n: [] for n in range(NQ)}
    for sender in range(NQ):
        for t in range(NQ):
            from_ = stat[t] if sender == 0 else stat_got[sender, t]
            found[seen_as(sender, t)].append((from_[0:1], from_[1:2]))
    log_totals = []
    for n in range(NQ):
        best = functools.reduce(jnp.maximum, [top for top, _ in found[n]])
        total = sum(part_total * jnp.exp2(top - best) for top, part_total in found[n])
        log_totals.append(best + jnp.log2(total))
    lines = []
    for source in (stat_first, stat):
        for t in range(NQ):
            line = jnp.exp2(source[t, 0:1, :] - log_totals[t])
            for h in range(heads):
                lines.append(line[:, h * blk : (h + 1) * blk])
    lines.append(jnp.zeros((blk - 2 * NQ * heads, blk), F32))
    columns[...] = jnp.transpose(jnp.concatenate(lines, axis=0))
    weights = []
    for sender in range(NQ):
        t = [n for n in range(NQ) if seen_as(sender, n) == 0][0]
        top = stat[t, 0:1, :] if sender == 0 else stat_got[sender, t, 0:1, :]
        weights.append(jnp.exp2(top - log_totals[0]) * factor)

    def scaled_rows(half):
        for t in range(NQ):
            for h in range(heads):
                n = t * heads + h
                c = columns[:, half * NQ * heads + n : half * NQ * heads + n + 1]
                place = slice(n * blk, (n + 1) * blk)
                lanes = slice(h * dh, (h + 1) * dh)
                qc[place, :] = (qs[t, :, lanes].astype(F32) * c).astype(BF16)
                gc[place, :] = (gs[t, :, lanes].astype(F32) * c).astype(BF16)

    def key_grads(first):
        rows = slice(first * blk, (first + 4) * blk)
        dv = jnp.dot(probs[rows, :], gc[...], preferred_element_type=F32)
        dk = jnp.dot(dscores[rows, :], qc[...], preferred_element_type=F32) * factor
        for n in range(4):
            j = first + n
            part[j, 0] = dk[n * blk : (n + 1) * blk].astype(BF16)
            part[j, 1] = dv[n * blk : (n + 1) * blk].astype(BF16)
            if j > 0:
                p_copy(j).start()

    scaled_rows(1)
    key_grads(8)
    key_grads(12)
    scaled_rows(0)
    key_grads(4)
    key_grads(0)

    for t in range(1, NQ):
        u_copy(t).wait_recv()
    for h in range(heads):
        lanes = slice(h * blk, (h + 1) * blk)
        acc = weights[0][:, lanes] * u_mine[0, :, lanes].astype(F32)
        for t in range(1, NQ):
            acc += weights[t][:, lanes] * u_got[t, :, lanes].astype(F32)
        dq_out[:, h * dh : (h + 1) * dh] = jnp.transpose(acc).astype(BF16)

    for j in range(1, NK):
        p_copy(j).wait_recv()
    dk_sum = part[0, 0].astype(F32)
    dv_sum = part[0, 1].astype(F32)
    for j in range(1, NK):
        dk_sum += part_got[j, 0].astype(F32)
        dv_sum += part_got[j, 1].astype(F32)
    dk_out[...] = dk_sum.astype(BF16)
    dv_out[...] = dv_sum.astype(BF16)

    for j in range(1, NK):
        for copy in k_copy(j):
            copy.wait_send()
        p_copy(j).wait_send()
    for t in range(1, NQ):
        for copy in q_copy(q_in, g_in, t, query_reader(t)):
            copy.wait_send()
        d_copy(t).wait_send()
        u_copy(t).wait_send()
        for batch in range(2):
            s_copy(t, batch).wait_send()


def per_device(queries, keys, values, outputs, grad_out, block_order):
    anywhere = pl.BlockSpec(memory_space=pl.ANY)
    whole = pl.BlockSpec(memory_space=pltpu.VMEM)
    dma = pltpu.SemaphoreType.DMA
    return pl.pallas_call(
        kernel,
        out_shape=(
            jax.ShapeDtypeStruct((128, 512), BF16),
            jax.ShapeDtypeStruct((128, 128), BF16),
            jax.ShapeDtypeStruct((128, 128), BF16),
        ),
        in_specs=[pl.BlockSpec(memory_space=pltpu.SMEM)] + [anywhere] * 5,
        out_specs=(whole, whole, whole),
        scratch_shapes=[
            pltpu.VMEM((NQ, 128, 512), BF16),
            pltpu.VMEM((NQ, 128, 512), BF16),
            pltpu.VMEM((128, 512), BF16),
            pltpu.VMEM((NQ, 1, 512), F32),
            pltpu.VMEM((2048, 128), BF16),
            pltpu.VMEM((2048, 128), BF16),
            pltpu.VMEM((128, 2048), BF16),
            pltpu.VMEM((HALF, 256), F32),
            pltpu.VMEM((2048, 4096), BF16),
            pltpu.VMEM((2048, 4096), BF16),
            pltpu.VMEM((NQ, 128, 512), F32),
            pltpu.VMEM((NQ, 128, 512), BF16),
            pltpu.VMEM((NQ, 128, 512), BF16),
            pltpu.VMEM((NQ, 2, 512), F32),
            pltpu.VMEM((NQ, 2, 512), F32),
            pltpu.VMEM((NQ, NQ, 2, 512), F32),
            pltpu.VMEM((128, 128), F32),
            pltpu.VMEM((4096, 128), BF16),
            pltpu.VMEM((4096, 128), BF16),
            pltpu.VMEM((NK, 2, 128, 128), BF16),
            pltpu.VMEM((NK, 2, 128, 128), BF16),
            dma((5,)),
            dma((NQ, 2)),
            dma((NQ, 2)),
            dma((NQ,)),
            dma((NQ,)),
            dma((NK, 2)),
            dma((NK, 2)),
            dma((NQ,)),
            dma((NQ,)),
            dma((NQ, 2)),
            dma((NQ, 2)),
            dma((NK,)),
            dma((NK,)),
        ],
        compiler_params=pltpu.CompilerParams(
            collective_id=0, has_side_effects=True, vmem_limit_bytes=60 * 1024 * 1024
        ),
        name="attention_backward",
    )(block_order, queries, keys, values, outputs, grad_out)


def solution(mesh):
    rows = P(("row", "col"), None)
    return jax.shard_map(
        per_device,
        mesh=mesh,
        in_specs=(rows, rows, rows, rows, rows, P()),
        out_specs=(rows, rows, rows),
        check_vma=False,
    )
```

```python
import functools
import math

import jax
import jax.numpy as jnp
from jax import lax
from jax.experimental import pallas as pl
from jax.experimental.pallas import tpu as pltpu
from jax.sharding import PartitionSpec as P

MESH = pl.DeviceIdType.MESH
F32 = jnp.float32
BF16 = jnp.bfloat16
HIDDEN = -1e30

NQ = 8
NK = 16
KEY_STEPS = (
    ((0, 0), (1, 0), (3, 0), (0, 1), (0, 3), (1, 1), (3, 3), (1, 3))
    + ((2, 1), (2, 3), (1, 2), (3, 2), (2, 0), (0, 2), (2, 2), (3, 1))
)
NEAR = (1, 2, 3, 4, 5, 6, 7, 15)
FAR = (12, 13, 8, 9, 10, 11)
CORNER = 14
HALF = 1024


def here():
    row = lax.axis_index("row")
    col = lax.axis_index("col")
    z = (row // 8) * 2 + col // 4
    return (row // 2) % 4, col % 4, z, row % 2


def device(x, y, z, core):
    return (((z // 2) * 4 + x) * 2 + core, (z % 2) * 4 + y)


def y_step(t):
    u = t // 2
    return u + (u // 2) * (5 - 2 * u)


def query_owner(t):
    x, y, z, core = here()
    return x, (y + 4 - y_step(t)) % 4, z, (core + t % 2) % 2


def query_reader(t):
    x, y, z, core = here()
    return x, (y + y_step(t)) % 4, z, (core + t % 2) % 2


def key_owner(j):
    x, y, z, core = here()
    dx, dz = KEY_STEPS[j]
    return (x + 4 - dx) % 4, y, (z + 4 - dz) % 4, core


def key_reader(j):
    x, y, z, core = here()
    dx, dz = KEY_STEPS[j]
    return (x + dx) % 4, y, (z + dz) % 4, core


def key_step(j, part):
    size = 1 if part == 0 else 3
    dx, dz = KEY_STEPS[j]
    return (size, 0) if dx == 2 else (0, size)


def halfway(j, part):
    step = key_step(j, part)
    dx, dz = KEY_STEPS[j]
    return KEY_STEPS.index(((dx - step[0]) % 4, (dz - step[1]) % 4))


def neighbour(step, sign):
    x, y, z, core = here()
    return (x + 4 + sign * step[0]) % 4, y, (z + 4 + sign * step[1]) % 4, core


def static_y(t):
    return (0, 1, 3, 2)[t // 2]


def seen_as(sender, t):
    dy = (static_y(t) - static_y(sender)) % 4
    return 2 * (0, 1, 3, 2)[dy] + (sender + t) % 2


def slot_of(place):
    row, col = device(*place)
    return row * 8 + col


def kernel(
    order,
    q_in,
    k_in,
    v_in,
    o_in,
    g_in,
    dq_out,
    dk_out,
    dv_out,
    qs,
    gs,
    own_o,
    delta,
    ks,
    vs,
    kt,
    scores,
    probs,
    dscores,
    u_sum,
    u_mine,
    u_got,
    stat_first,
    stat,
    stat_got,
    columns,
    qc,
    gc,
    part,
    part_got,
    relayed,
    local_sem,
    q_send,
    q_recv,
    d_send,
    d_recv,
    k_send,
    k_recv,
    u_send,
    u_recv,
    s_send,
    s_recv,
    p_send,
    p_recv,
    r_send,
    r_recv,
):
    dh = 128
    blk = 128
    heads = 4
    factor = 1.0 / math.sqrt(dh)
    scale2 = factor * math.log2(math.e)

    def remote(src, dst, send, recv, place):
        return pltpu.make_async_remote_copy(
            src_ref=src,
            dst_ref=dst,
            send_sem=send,
            recv_sem=recv,
            device_id=device(*place),
            device_id_type=MESH,
        )

    def q_copy(src_q, src_g, t, place):
        return (
            remote(src_q, qs.at[t], q_send.at[t, 0], q_recv.at[t, 0], place),
            remote(src_g, gs.at[t], q_send.at[t, 1], q_recv.at[t, 1], place),
        )

    def k_copy(j):
        rows = pl.ds(j * blk, blk)
        return (
            remote(k_in, ks.at[rows], k_send.at[j, 0], k_recv.at[j, 0], key_reader(j)),
            remote(v_in, vs.at[rows], k_send.at[j, 1], k_recv.at[j, 1], key_reader(j)),
        )

    def relay_keys(j, part):
        ref = (ks, vs)[part]
        return remote(
            ref.at[pl.ds(halfway(j, part) * blk, blk)],
            ref.at[pl.ds(j * blk, blk)],
            k_send.at[j, part],
            k_recv.at[j, part],
            neighbour(key_step(j, part), 1),
        )

    def relay_grads(j, part_):
        return remote(
            part.at[j, part_],
            relayed.at[j - 8, part_],
            r_send.at[j - 8, part_],
            r_recv.at[j - 8, part_],
            neighbour(key_step(j, part_), -1),
        )

    def d_copy(t):
        return remote(delta.at[0], delta.at[t], d_send.at[t], d_recv.at[t], query_reader(t))

    def u_copy(t):
        return remote(u_mine.at[t], u_got.at[t], u_send.at[t], u_recv.at[t], query_owner(t))

    def s_copy(t, batch):
        some = pl.ds(batch * 4, 4)
        return remote(
            stat.at[some],
            stat_got.at[t, some],
            s_send.at[t, batch],
            s_recv.at[t, batch],
            query_owner(t),
        )

    def p_copy(j):
        return remote(part.at[j], part_got.at[j], p_send.at[j], p_recv.at[j], key_owner(j))

    barrier = pltpu.get_barrier_semaphore()
    for t in range(1, NQ):
        pl.semaphore_signal(barrier, inc=1, device_id=device(*query_reader(t)), device_id_type=MESH)
    for j in NEAR + (CORNER,):
        pl.semaphore_signal(barrier, inc=1, device_id=device(*key_reader(j)), device_id_type=MESH)
    locals_ = [
        pltpu.make_async_copy(o_in, own_o, local_sem.at[0]),
        pltpu.make_async_copy(g_in, gs.at[0], local_sem.at[1]),
        pltpu.make_async_copy(q_in, qs.at[0], local_sem.at[2]),
        pltpu.make_async_copy(k_in, ks.at[pl.ds(0, blk)], local_sem.at[3]),
        pltpu.make_async_copy(v_in, vs.at[pl.ds(0, blk)], local_sem.at[4]),
    ]
    for copy in locals_:
        copy.start()
    for copy in locals_:
        copy.wait()
    product = gs[0].astype(F32) * own_o[...].astype(F32)
    for h in range(heads):
        summed = jnp.sum(product[:, h * dh : (h + 1) * dh], axis=1, keepdims=True)
        wide = jnp.broadcast_to(summed, (blk, dh))
        delta[0, :, h * blk : (h + 1) * blk] = jnp.transpose(wide)[0:1, :]
    pl.semaphore_wait(barrier, NQ - 1 + len(NEAR) + 1)

    def start_keys(slots):
        for j in slots:
            for copy in k_copy(j):
                copy.start()

    start_keys(NEAR)
    for t in (1, 2, 4):
        for copy in q_copy(q_in, g_in, t, query_reader(t)):
            copy.start()
    for t in range(1, NQ):
        d_copy(t).start()
    start_keys((CORNER,))
    for copy in q_copy(q_in, g_in, 6, query_reader(6)):
        copy.start()

    def turn_keys(slots):
        for j in slots:
            kt[:, j * blk : (j + 1) * blk] = jnp.transpose(
                ks[j * blk : (j + 1) * blk, :].astype(F32)
            ).astype(BF16)

    x, y, z, core = here()
    row_less_col = lax.broadcasted_iota(jnp.int32, (blk, 2 * blk), 0) - (
        lax.broadcasted_iota(jnp.int32, (blk, 2 * blk), 1) % blk
    )
    chunk = 512
    per_chunk = chunk // blk

    def unit(t, half, with_u):
        q_order = order[slot_of(query_owner(t))]
        slots = range(half * 8, half * 8 + 8)
        penalty = {}
        for j in slots[1 - half :]:
            k_order = order[slot_of(key_owner(j))]
            penalty[j] = jnp.where(k_order < q_order, 0.0, -HIDDEN).astype(F32)

        def two_heads(ref, pair):
            return jnp.concatenate(
                [ref[t, :, (2 * pair + i) * dh : (2 * pair + i + 1) * dh] for i in range(2)], axis=0
            )

        def score_part(pair, q2, first, top8):
            rows = slice(first * blk, (first + per_chunk) * blk)
            s = lax.dot_general(
                ks[rows, :], q2, (((1,), (1,)), ((), ())), preferred_element_type=F32
            )
            for i in range(per_chunk):
                j = first + i
                n = j - half * 8
                tile = s[i * blk : (i + 1) * blk]
                if j == 0:
                    k_order = order[slot_of(key_owner(0))]
                    tile = jnp.where(row_less_col <= blk * (q_order - k_order), tile, HIDDEN)
                scores[pair, n * blk : (n + 1) * blk, :] = tile
                largest = jnp.max(tile.reshape(blk // 8, 8, 256), axis=0)
                top8 = jnp.maximum(top8, largest - penalty[j] if j > 0 else largest)
            return top8

        def grad_part(pair, g2, first, top, away, total8):
            lanes = pl.ds(pl.multiple_of(t * 512 + pair * 256, 256), 256)
            rows = slice(first * blk, (first + per_chunk) * blk)
            dp = lax.dot_general(
                vs[rows, :], g2, (((1,), (1,)), ((), ())), preferred_element_type=F32
            )
            for i in range(per_chunk):
                j = first + i
                n = j - half * 8
                tile_rows = slice(j * blk, (j + 1) * blk)
                shift = top + penalty[j] if j > 0 else top
                p = jnp.exp2(scores[pair, n * blk : (n + 1) * blk, :] * scale2 - shift)
                total8 += jnp.sum(p.reshape(blk // 8, 8, 256), axis=0)
                ds = p * (dp[i * blk : (i + 1) * blk] - away)
                probs[tile_rows, lanes] = p.astype(BF16)
                dscores[tile_rows, lanes] = ds.astype(BF16)
            return total8

        queries = [two_heads(qs, pair) for pair in range(2)]
        top8 = [jnp.full((8, 256), HIDDEN, F32) for pair in range(2)]
        for first in slots[::per_chunk]:
            top8[0] = score_part(0, queries[0], first, top8[0])
        for pair in range(2):
            own = slice(pair * 256, pair * 256 + 256)
            top = jnp.max(top8[pair], axis=0, keepdims=True) * scale2
            if half == 1:
                before = stat_first[t, 0:1, own]
                top = jnp.maximum(top, before)
            total8 = jnp.zeros((8, 256), F32)
            g2 = two_heads(gs, pair)
            away = delta[t, :, own]
            for first in slots[::per_chunk]:
                if pair == 0:
                    top8[1] = score_part(1, queries[1], first, top8[1])
                total8 = grad_part(pair, g2, first, top, away, total8)
            total = jnp.sum(total8, axis=0, keepdims=True)
            if with_u:
                lanes = pl.ds(pl.multiple_of(t * 512 + pair * 256, 256), 256)
                keys_ = slice(half * HALF, (half + 1) * HALF)
                du = jnp.dot(kt[:, keys_], dscores[keys_, lanes], preferred_element_type=F32)
            if half == 0:
                stat_first[t, 0:1, own] = top
                stat_first[t, 1:2, own] = total
                u_sum[t, :, own] = du
            else:
                shrink = jnp.exp2(before - top)
                stat[t, 0:1, own] = top
                stat[t, 1:2, own] = total + stat_first[t, 1:2, own] * shrink
                if with_u:
                    u_mine[t, :, own] = (du + u_sum[t, :, own] * shrink).astype(BF16)

    def first_half(t, carry):
        @pl.when(t > 0)
        def _():
            for copy in q_copy(q_in, g_in, t, query_reader(t)):
                copy.wait_recv()
            d_copy(t).wait_recv()

        @pl.when(jnp.logical_and(t > 1, t % 2 == 0))
        def _():
            for copy in q_copy(qs.at[t], gs.at[t], t + 1, (x, y, z, (core + 1) % 2)):
                copy.start()

        unit(t, 0, True)
        return carry

    def second_half(t, carry):
        unit(t, 1, True)

        @pl.when(t > 0)
        def _():
            u_copy(t).start()

        return carry

    def second_half_late(t, carry):
        unit(t, 1, False)
        return carry

    def late_u(t, carry):
        lanes = pl.ds(pl.multiple_of(t * 512, 512), 512)
        du = jnp.dot(kt[:, HALF:], dscores[HALF:, lanes], preferred_element_type=F32)
        shrink = jnp.exp2(stat_first[t, 0:1, :] - stat[t, 0:1, :])
        u_mine[t] = (du + u_sum[t] * shrink).astype(BF16)
        u_copy(t).start()
        return carry

    for j in NEAR:
        for part_, copy in enumerate(k_copy(j)):
            copy.wait_recv()
            for far in FAR:
                if halfway(far, part_) == j:
                    relay_keys(far, part_).start()
    turn_keys(range(8))
    lax.fori_loop(0, NQ, first_half, 0)
    for j in FAR + (CORNER,):
        for copy in k_copy(j):
            copy.wait_recv()
    turn_keys(range(8, NK))
    lax.fori_loop(0, 4, second_half, 0)
    for t in range(1, NQ):
        s_copy(t, 0).start()
    lax.fori_loop(4, NQ, second_half_late, 0)
    for t in range(1, NQ):
        s_copy(t, 1).start()
    lax.fori_loop(4, NQ, late_u, 0)

    for t in range(1, NQ):
        for batch in range(2):
            s_copy(t, batch).wait_recv()
    found = {n: [] for n in range(NQ)}
    for sender in range(NQ):
        for t in range(NQ):
            from_ = stat[t] if sender == 0 else stat_got[sender, t]
            found[seen_as(sender, t)].append((from_[0:1], from_[1:2]))
    log_totals = []
    for n in range(NQ):
        best = functools.reduce(jnp.maximum, [top for top, _ in found[n]])
        total = sum(part_total * jnp.exp2(top - best) for top, part_total in found[n])
        log_totals.append(best + jnp.log2(total))
    lines = []
    for source in (stat_first, stat):
        for t in range(NQ):
            line = jnp.exp2(source[t, 0:1, :] - log_totals[t])
            for h in range(heads):
                lines.append(line[:, h * blk : (h + 1) * blk])
    lines.append(jnp.zeros((blk - 2 * NQ * heads, blk), F32))
    columns[...] = jnp.transpose(jnp.concatenate(lines, axis=0))
    weights = []
    for sender in range(NQ):
        t = [n for n in range(NQ) if seen_as(sender, n) == 0][0]
        top = stat[t, 0:1, :] if sender == 0 else stat_got[sender, t, 0:1, :]
        weights.append(jnp.exp2(top - log_totals[0]) * factor)

    def scaled_rows(half):
        for t in range(NQ):
            for h in range(heads):
                n = t * heads + h
                c = columns[:, half * NQ * heads + n : half * NQ * heads + n + 1]
                place = slice(n * blk, (n + 1) * blk)
                lanes = slice(h * dh, (h + 1) * dh)
                qc[place, :] = (qs[t, :, lanes].astype(F32) * c).astype(BF16)
                gc[place, :] = (gs[t, :, lanes].astype(F32) * c).astype(BF16)

    def key_grads(first):
        rows = slice(first * blk, (first + 4) * blk)
        dv = jnp.dot(probs[rows, :], gc[...], preferred_element_type=F32)
        dk = jnp.dot(dscores[rows, :], qc[...], preferred_element_type=F32) * factor
        for n in range(4):
            j = first + n
            part[j, 0] = dk[n * blk : (n + 1) * blk].astype(BF16)
            part[j, 1] = dv[n * blk : (n + 1) * blk].astype(BF16)

    def send_near(slots):
        for j in slots:
            for part_ in range(2):
                total = part[j, part_].astype(F32)
                extra = [far for far in FAR if halfway(far, part_) == j]
                for far in extra:
                    relay_grads(far, part_).wait_recv()
                    total += relayed[far - 8, part_].astype(F32)
                if extra:
                    part[j, part_] = total.astype(BF16)
            p_copy(j).start()

    scaled_rows(1)
    key_grads(8)
    for j in (8, 9, 10, 11):
        for part_ in range(2):
            relay_grads(j, part_).start()
    key_grads(12)
    for j in (12, 13):
        for part_ in range(2):
            relay_grads(j, part_).start()
    p_copy(CORNER).start()
    scaled_rows(0)
    key_grads(4)
    send_near((5, 6, 7, 15))
    key_grads(0)
    send_near((1, 2, 3, 4))

    for t in range(1, NQ):
        u_copy(t).wait_recv()
    for h in range(heads):
        lanes = slice(h * blk, (h + 1) * blk)
        acc = weights[0][:, lanes] * u_mine[0, :, lanes].astype(F32)
        for t in range(1, NQ):
            acc += weights[t][:, lanes] * u_got[t, :, lanes].astype(F32)
        dq_out[:, h * dh : (h + 1) * dh] = jnp.transpose(acc).astype(BF16)

    dk_sum = part[0, 0].astype(F32)
    dv_sum = part[0, 1].astype(F32)
    for j in (CORNER, 5, 6, 7, 15, 1, 2, 3, 4):
        p_copy(j).wait_recv()
        dk_sum += part_got[j, 0].astype(F32)
        dv_sum += part_got[j, 1].astype(F32)
    dk_out[...] = dk_sum.astype(BF16)
    dv_out[...] = dv_sum.astype(BF16)

    for j in NEAR + (CORNER,):
        for copy in k_copy(j):
            copy.wait_send()
        p_copy(j).wait_send()
    for j in FAR:
        for part_ in range(2):
            relay_keys(j, part_).wait_send()
            relay_grads(j, part_).wait_send()
    for t in range(1, NQ):
        for copy in q_copy(q_in, g_in, t, query_reader(t)):
            copy.wait_send()
        d_copy(t).wait_send()
        u_copy(t).wait_send()
        for batch in range(2):
            s_copy(t, batch).wait_send()


def per_device(queries, keys, values, outputs, grad_out, block_order):
    anywhere = pl.BlockSpec(memory_space=pl.ANY)
    whole = pl.BlockSpec(memory_space=pltpu.VMEM)
    dma = pltpu.SemaphoreType.DMA
    return pl.pallas_call(
        kernel,
        out_shape=(
            jax.ShapeDtypeStruct((128, 512), BF16),
            jax.ShapeDtypeStruct((128, 128), BF16),
            jax.ShapeDtypeStruct((128, 128), BF16),
        ),
        in_specs=[pl.BlockSpec(memory_space=pltpu.SMEM)] + [anywhere] * 5,
        out_specs=(whole, whole, whole),
        scratch_shapes=[
            pltpu.VMEM((NQ, 128, 512), BF16),
            pltpu.VMEM((NQ, 128, 512), BF16),
            pltpu.VMEM((128, 512), BF16),
            pltpu.VMEM((NQ, 1, 512), F32),
            pltpu.VMEM((2048, 128), BF16),
            pltpu.VMEM((2048, 128), BF16),
            pltpu.VMEM((128, 2048), BF16),
            pltpu.VMEM((2, HALF, 256), F32),
            pltpu.VMEM((2048, 4096), BF16),
            pltpu.VMEM((2048, 4096), BF16),
            pltpu.VMEM((NQ, 128, 512), F32),
            pltpu.VMEM((NQ, 128, 512), BF16),
            pltpu.VMEM((NQ, 128, 512), BF16),
            pltpu.VMEM((NQ, 2, 512), F32),
            pltpu.VMEM((NQ, 2, 512), F32),
            pltpu.VMEM((NQ, NQ, 2, 512), F32),
            pltpu.VMEM((128, 128), F32),
            pltpu.VMEM((4096, 128), BF16),
            pltpu.VMEM((4096, 128), BF16),
            pltpu.VMEM((NK, 2, 128, 128), BF16),
            pltpu.VMEM((NK, 2, 128, 128), BF16),
            pltpu.VMEM((6, 2, 128, 128), BF16),
            dma((5,)),
            dma((NQ, 2)),
            dma((NQ, 2)),
            dma((NQ,)),
            dma((NQ,)),
            dma((NK, 2)),
            dma((NK, 2)),
            dma((NQ,)),
            dma((NQ,)),
            dma((NQ, 2)),
            dma((NQ, 2)),
            dma((NK,)),
            dma((NK,)),
            dma((6, 2)),
            dma((6, 2)),
        ],
        compiler_params=pltpu.CompilerParams(
            collective_id=0, has_side_effects=True, vmem_limit_bytes=60 * 1024 * 1024
        ),
        name="attention_backward",
    )(block_order, queries, keys, values, outputs, grad_out)


def solution(mesh):
    rows = P(("row", "col"), None)
    return jax.shard_map(
        per_device,
        mesh=mesh,
        in_specs=(rows, rows, rows, rows, rows, P()),
        out_specs=(rows, rows, rows),
        check_vma=False,
    )
```

```python
import functools
import math

import jax
import jax.numpy as jnp
from jax import lax
from jax.experimental import pallas as pl
from jax.experimental.pallas import tpu as pltpu
from jax.sharding import PartitionSpec as P

MESH = pl.DeviceIdType.MESH
F32 = jnp.float32
BF16 = jnp.bfloat16
HIDDEN = -1e30

NQ = 8
NK = 16
KEY_STEPS = (
    ((0, 0), (1, 0), (3, 0), (0, 1), (0, 3), (1, 1), (3, 3), (1, 3))
    + ((2, 1), (2, 3), (1, 2), (3, 2), (2, 0), (0, 2), (2, 2), (3, 1))
)
NEAR = (1, 2, 3, 4, 5, 6, 7, 15)
FAR = (12, 13, 8, 9, 10, 11)
CORNER = 14
HALF = 1024
STAT_BATCHES = ((6, 2), (0, 2), (2, 4))


def here():
    row = lax.axis_index("row")
    col = lax.axis_index("col")
    z = (row // 8) * 2 + col // 4
    return (row // 2) % 4, col % 4, z, row % 2


def device(x, y, z, core):
    return (((z // 2) * 4 + x) * 2 + core, (z % 2) * 4 + y)


def y_step(t):
    u = t // 2
    return u + (u // 2) * (5 - 2 * u)


def query_owner(t):
    x, y, z, core = here()
    return x, (y + 4 - y_step(t)) % 4, z, (core + t % 2) % 2


def query_reader(t):
    x, y, z, core = here()
    return x, (y + y_step(t)) % 4, z, (core + t % 2) % 2


def key_owner(j):
    x, y, z, core = here()
    dx, dz = KEY_STEPS[j]
    return (x + 4 - dx) % 4, y, (z + 4 - dz) % 4, core


def key_reader(j):
    x, y, z, core = here()
    dx, dz = KEY_STEPS[j]
    return (x + dx) % 4, y, (z + dz) % 4, core


def key_step(j, part):
    size = 1 if part == 0 else 3
    dx, dz = KEY_STEPS[j]
    return (size, 0) if dx == 2 else (0, size)


def halfway(j, part):
    step = key_step(j, part)
    dx, dz = KEY_STEPS[j]
    return KEY_STEPS.index(((dx - step[0]) % 4, (dz - step[1]) % 4))


def neighbour(step, sign):
    x, y, z, core = here()
    return (x + 4 + sign * step[0]) % 4, y, (z + 4 + sign * step[1]) % 4, core


def static_y(t):
    return (0, 1, 3, 2)[t // 2]


def seen_as(sender, t):
    dy = (static_y(t) - static_y(sender)) % 4
    return 2 * (0, 1, 3, 2)[dy] + (sender + t) % 2


def slot_of(place):
    row, col = device(*place)
    return row * 8 + col


def kernel(
    order,
    q_in,
    k_in,
    v_in,
    o_in,
    g_in,
    dq_out,
    dk_out,
    dv_out,
    qs,
    gs,
    own_o,
    delta,
    ks,
    vs,
    kt,
    scores,
    probs,
    dscores,
    u_sum,
    u_mine,
    u_got,
    stat_first,
    stat,
    stat_got,
    columns,
    qc,
    gc,
    part,
    part_got,
    relayed,
    local_sem,
    q_send,
    q_recv,
    d_send,
    d_recv,
    k_send,
    k_recv,
    u_send,
    u_recv,
    s_send,
    s_recv,
    p_send,
    p_recv,
    r_send,
    r_recv,
):
    dh = 128
    blk = 128
    heads = 4
    factor = 1.0 / math.sqrt(dh)
    scale2 = factor * math.log2(math.e)

    def remote(src, dst, send, recv, place):
        return pltpu.make_async_remote_copy(
            src_ref=src,
            dst_ref=dst,
            send_sem=send,
            recv_sem=recv,
            device_id=device(*place),
            device_id_type=MESH,
        )

    def q_copy(src_q, src_g, t, place):
        return (
            remote(src_q, qs.at[t], q_send.at[t, 0], q_recv.at[t, 0], place),
            remote(src_g, gs.at[t], q_send.at[t, 1], q_recv.at[t, 1], place),
        )

    def k_copy(j):
        rows = pl.ds(j * blk, blk)
        return (
            remote(k_in, ks.at[rows], k_send.at[j, 0], k_recv.at[j, 0], key_reader(j)),
            remote(v_in, vs.at[rows], k_send.at[j, 1], k_recv.at[j, 1], key_reader(j)),
        )

    def relay_keys(j, part):
        ref = (ks, vs)[part]
        return remote(
            ref.at[pl.ds(halfway(j, part) * blk, blk)],
            ref.at[pl.ds(j * blk, blk)],
            k_send.at[j, part],
            k_recv.at[j, part],
            neighbour(key_step(j, part), 1),
        )

    def relay_grads(j, part_):
        return remote(
            part.at[j, part_],
            relayed.at[j - 8, part_],
            r_send.at[j - 8, part_],
            r_recv.at[j - 8, part_],
            neighbour(key_step(j, part_), -1),
        )

    def d_copy(t):
        return remote(delta.at[0], delta.at[t], d_send.at[t], d_recv.at[t], query_reader(t))

    def u_copy(t):
        return remote(u_mine.at[t], u_got.at[t], u_send.at[t], u_recv.at[t], query_owner(t))

    def s_copy(t, batch):
        some = pl.ds(*STAT_BATCHES[batch])
        return remote(
            stat.at[some],
            stat_got.at[t, some],
            s_send.at[t, batch],
            s_recv.at[t, batch],
            query_owner(t),
        )

    def p_copy(j):
        return remote(part.at[j], part_got.at[j], p_send.at[j], p_recv.at[j], key_owner(j))

    barrier = pltpu.get_barrier_semaphore()
    for t in range(1, NQ):
        pl.semaphore_signal(barrier, inc=1, device_id=device(*query_reader(t)), device_id_type=MESH)
    for j in NEAR + (CORNER,):
        pl.semaphore_signal(barrier, inc=1, device_id=device(*key_reader(j)), device_id_type=MESH)
    locals_ = [
        pltpu.make_async_copy(o_in, own_o, local_sem.at[0]),
        pltpu.make_async_copy(g_in, gs.at[0], local_sem.at[1]),
        pltpu.make_async_copy(q_in, qs.at[0], local_sem.at[2]),
        pltpu.make_async_copy(k_in, ks.at[pl.ds(0, blk)], local_sem.at[3]),
        pltpu.make_async_copy(v_in, vs.at[pl.ds(0, blk)], local_sem.at[4]),
    ]
    for copy in locals_:
        copy.start()
    for copy in locals_:
        copy.wait()
    product = gs[0].astype(F32) * own_o[...].astype(F32)
    for h in range(heads):
        summed = jnp.sum(product[:, h * dh : (h + 1) * dh], axis=1, keepdims=True)
        wide = jnp.broadcast_to(summed, (blk, dh))
        delta[0, :, h * blk : (h + 1) * blk] = jnp.transpose(wide)[0:1, :]
    pl.semaphore_wait(barrier, NQ - 1 + len(NEAR) + 1)

    def start_keys(slots):
        for j in slots:
            for copy in k_copy(j):
                copy.start()

    start_keys(NEAR)
    for t in (1, 2, 4):
        for copy in q_copy(q_in, g_in, t, query_reader(t)):
            copy.start()
    for t in range(1, NQ):
        d_copy(t).start()
    start_keys((CORNER,))
    for copy in q_copy(q_in, g_in, 6, query_reader(6)):
        copy.start()

    def turn_keys(slots):
        for j in slots:
            kt[:, j * blk : (j + 1) * blk] = jnp.transpose(
                ks[j * blk : (j + 1) * blk, :].astype(F32)
            ).astype(BF16)

    x, y, z, core = here()
    row_less_col = lax.broadcasted_iota(jnp.int32, (blk, 2 * blk), 0) - (
        lax.broadcasted_iota(jnp.int32, (blk, 2 * blk), 1) % blk
    )
    chunk = 512
    per_chunk = chunk // blk

    def unit(t, half, with_u):
        q_order = order[slot_of(query_owner(t))]
        slots = range(half * 8, half * 8 + 8)
        penalty = {}
        for j in slots[1 - half :]:
            k_order = order[slot_of(key_owner(j))]
            penalty[j] = jnp.where(k_order < q_order, 0.0, -HIDDEN).astype(F32)

        def two_heads(ref, pair):
            return jnp.concatenate(
                [ref[t, :, (2 * pair + i) * dh : (2 * pair + i + 1) * dh] for i in range(2)], axis=0
            )

        def score_part(pair, q2, first, top8):
            rows = slice(first * blk, (first + per_chunk) * blk)
            s = lax.dot_general(
                ks[rows, :], q2, (((1,), (1,)), ((), ())), preferred_element_type=F32
            )
            for i in range(per_chunk):
                j = first + i
                n = j - half * 8
                tile = s[i * blk : (i + 1) * blk]
                if j == 0:
                    k_order = order[slot_of(key_owner(0))]
                    tile = jnp.where(row_less_col <= blk * (q_order - k_order), tile, HIDDEN)
                scores[pair, n * blk : (n + 1) * blk, :] = tile
                largest = jnp.max(tile.reshape(blk // 8, 8, 256), axis=0)
                top8 = jnp.maximum(top8, largest - penalty[j] if j > 0 else largest)
            return top8

        def grad_part(pair, g2, first, top, away, total8):
            lanes = pl.ds(pl.multiple_of(t * 512 + pair * 256, 256), 256)
            rows = slice(first * blk, (first + per_chunk) * blk)
            dp = lax.dot_general(
                vs[rows, :], g2, (((1,), (1,)), ((), ())), preferred_element_type=F32
            )
            for i in range(per_chunk):
                j = first + i
                n = j - half * 8
                tile_rows = slice(j * blk, (j + 1) * blk)
                shift = top + penalty[j] if j > 0 else top
                p = jnp.exp2(scores[pair, n * blk : (n + 1) * blk, :] * scale2 - shift)
                total8 += jnp.sum(p.reshape(blk // 8, 8, 256), axis=0)
                ds = p * (dp[i * blk : (i + 1) * blk] - away)
                probs[tile_rows, lanes] = p.astype(BF16)
                dscores[tile_rows, lanes] = ds.astype(BF16)
            return total8

        queries = [two_heads(qs, pair) for pair in range(2)]
        top8 = [jnp.full((8, 256), HIDDEN, F32) for pair in range(2)]
        for first in slots[::per_chunk]:
            top8[0] = score_part(0, queries[0], first, top8[0])
        for pair in range(2):
            own = slice(pair * 256, pair * 256 + 256)
            top = jnp.max(top8[pair], axis=0, keepdims=True) * scale2
            if half == 1:
                before = stat_first[t, 0:1, own]
                top = jnp.maximum(top, before)
            total8 = jnp.zeros((8, 256), F32)
            g2 = two_heads(gs, pair)
            away = delta[t, :, own]
            for first in slots[::per_chunk]:
                if pair == 0:
                    top8[1] = score_part(1, queries[1], first, top8[1])
                total8 = grad_part(pair, g2, first, top, away, total8)
            total = jnp.sum(total8, axis=0, keepdims=True)
            if with_u:
                lanes = pl.ds(pl.multiple_of(t * 512 + pair * 256, 256), 256)
                keys_ = slice(half * HALF, (half + 1) * HALF)
                du = jnp.dot(kt[:, keys_], dscores[keys_, lanes], preferred_element_type=F32)
            if half == 0:
                stat_first[t, 0:1, own] = top
                stat_first[t, 1:2, own] = total
                u_sum[t, :, own] = du
            else:
                shrink = jnp.exp2(before - top)
                stat[t, 0:1, own] = top
                stat[t, 1:2, own] = total + stat_first[t, 1:2, own] * shrink
                if with_u:
                    u_mine[t, :, own] = (du + u_sum[t, :, own] * shrink).astype(BF16)

    def first_half(t, carry):
        @pl.when(t > 0)
        def _():
            for copy in q_copy(q_in, g_in, t, query_reader(t)):
                copy.wait_recv()
            d_copy(t).wait_recv()

        @pl.when(jnp.logical_and(t > 1, t % 2 == 0))
        def _():
            for copy in q_copy(qs.at[t], gs.at[t], t + 1, (x, y, z, (core + 1) % 2)):
                copy.start()

        unit(t, 0, True)
        return carry

    def second_half(i, carry):
        t = (i + 6) % NQ
        unit(t, 1, True)

        @pl.when(t > 0)
        def _():
            u_copy(t).start()

        return carry

    def second_half_late(t, carry):
        unit(t, 1, False)
        return carry

    def late_u(t, carry):
        lanes = pl.ds(pl.multiple_of(t * 512, 512), 512)
        du = jnp.dot(kt[:, HALF:], dscores[HALF:, lanes], preferred_element_type=F32)
        shrink = jnp.exp2(stat_first[t, 0:1, :] - stat[t, 0:1, :])
        u_mine[t] = (du + u_sum[t] * shrink).astype(BF16)
        u_copy(t).start()
        return carry

    for j in NEAR:
        for part_, copy in enumerate(k_copy(j)):
            copy.wait_recv()
            for far in FAR:
                if halfway(far, part_) == j:
                    relay_keys(far, part_).start()
    turn_keys(range(8))
    lax.fori_loop(0, NQ, first_half, 0)
    for j in FAR + (CORNER,):
        for copy in k_copy(j):
            copy.wait_recv()
    turn_keys(range(8, NK))
    lax.fori_loop(0, 4, second_half, 0)
    for t in range(1, NQ):
        s_copy(t, 0).start()
        s_copy(t, 1).start()
    lax.fori_loop(2, 6, second_half_late, 0)
    for t in range(1, NQ):
        s_copy(t, 2).start()
    lax.fori_loop(2, 6, late_u, 0)

    for t in range(1, NQ):
        for batch in range(len(STAT_BATCHES)):
            s_copy(t, batch).wait_recv()
    found = {n: [] for n in range(NQ)}
    for sender in range(NQ):
        for t in range(NQ):
            from_ = stat[t] if sender == 0 else stat_got[sender, t]
            found[seen_as(sender, t)].append((from_[0:1], from_[1:2]))
    log_totals = []
    for n in range(NQ):
        best = functools.reduce(jnp.maximum, [top for top, _ in found[n]])
        total = sum(part_total * jnp.exp2(top - best) for top, part_total in found[n])
        log_totals.append(best + jnp.log2(total))
    lines = []
    for source in (stat_first, stat):
        for t in range(NQ):
            line = jnp.exp2(source[t, 0:1, :] - log_totals[t])
            for h in range(heads):
                lines.append(line[:, h * blk : (h + 1) * blk])
    lines.append(jnp.zeros((blk - 2 * NQ * heads, blk), F32))
    columns[...] = jnp.transpose(jnp.concatenate(lines, axis=0))
    weights = []
    for sender in range(NQ):
        t = [n for n in range(NQ) if seen_as(sender, n) == 0][0]
        top = stat[t, 0:1, :] if sender == 0 else stat_got[sender, t, 0:1, :]
        weights.append(jnp.exp2(top - log_totals[0]) * factor)

    def scaled_rows(half):
        for t in range(NQ):
            for h in range(heads):
                n = t * heads + h
                c = columns[:, half * NQ * heads + n : half * NQ * heads + n + 1]
                place = slice(n * blk, (n + 1) * blk)
                lanes = slice(h * dh, (h + 1) * dh)
                qc[place, :] = (qs[t, :, lanes].astype(F32) * c).astype(BF16)
                gc[place, :] = (gs[t, :, lanes].astype(F32) * c).astype(BF16)

    def key_grads(first, count):
        rows = slice(first * blk, (first + count) * blk)
        dv = jnp.dot(probs[rows, :], gc[...], preferred_element_type=F32)
        dk = jnp.dot(dscores[rows, :], qc[...], preferred_element_type=F32) * factor
        for n in range(count):
            j = first + n
            part[j, 0] = dk[n * blk : (n + 1) * blk].astype(BF16)
            part[j, 1] = dv[n * blk : (n + 1) * blk].astype(BF16)

    def send_near(slots):
        for j in slots:
            for part_ in range(2):
                total = part[j, part_].astype(F32)
                extra = [far for far in FAR if halfway(far, part_) == j]
                for far in extra:
                    relay_grads(far, part_).wait_recv()
                    total += relayed[far - 8, part_].astype(F32)
                if extra:
                    part[j, part_] = total.astype(BF16)
            p_copy(j).start()

    scaled_rows(1)
    key_grads(8, 4)
    for j in (8, 9, 10, 11):
        for part_ in range(2):
            relay_grads(j, part_).start()
    key_grads(12, 4)
    for j in (12, 13):
        for part_ in range(2):
            relay_grads(j, part_).start()
    p_copy(CORNER).start()
    scaled_rows(0)
    key_grads(4, 4)
    send_near((5, 6, 7, 15, 4))
    key_grads(1, 3)
    send_near((1, 2, 3))
    key_grads(0, 1)

    for t in range(1, NQ):
        u_copy(t).wait_recv()
    for h in range(heads):
        lanes = slice(h * blk, (h + 1) * blk)
        acc = weights[0][:, lanes] * u_mine[0, :, lanes].astype(F32)
        for t in range(1, NQ):
            acc += weights[t][:, lanes] * u_got[t, :, lanes].astype(F32)
        dq_out[:, h * dh : (h + 1) * dh] = jnp.transpose(acc).astype(BF16)

    dk_sum = part[0, 0].astype(F32)
    dv_sum = part[0, 1].astype(F32)
    for j in (CORNER, 5, 6, 7, 15, 1, 2, 3, 4):
        p_copy(j).wait_recv()
        dk_sum += part_got[j, 0].astype(F32)
        dv_sum += part_got[j, 1].astype(F32)
    dk_out[...] = dk_sum.astype(BF16)
    dv_out[...] = dv_sum.astype(BF16)

    for j in NEAR + (CORNER,):
        for copy in k_copy(j):
            copy.wait_send()
        p_copy(j).wait_send()
    for j in FAR:
        for part_ in range(2):
            relay_keys(j, part_).wait_send()
            relay_grads(j, part_).wait_send()
    for t in range(1, NQ):
        for copy in q_copy(q_in, g_in, t, query_reader(t)):
            copy.wait_send()
        d_copy(t).wait_send()
        u_copy(t).wait_send()
        for batch in range(len(STAT_BATCHES)):
            s_copy(t, batch).wait_send()


def per_device(queries, keys, values, outputs, grad_out, block_order):
    anywhere = pl.BlockSpec(memory_space=pl.ANY)
    whole = pl.BlockSpec(memory_space=pltpu.VMEM)
    dma = pltpu.SemaphoreType.DMA
    return pl.pallas_call(
        kernel,
        out_shape=(
            jax.ShapeDtypeStruct((128, 512), BF16),
            jax.ShapeDtypeStruct((128, 128), BF16),
            jax.ShapeDtypeStruct((128, 128), BF16),
        ),
        in_specs=[pl.BlockSpec(memory_space=pltpu.SMEM)] + [anywhere] * 5,
        out_specs=(whole, whole, whole),
        scratch_shapes=[
            pltpu.VMEM((NQ, 128, 512), BF16),
            pltpu.VMEM((NQ, 128, 512), BF16),
            pltpu.VMEM((128, 512), BF16),
            pltpu.VMEM((NQ, 1, 512), F32),
            pltpu.VMEM((2048, 128), BF16),
            pltpu.VMEM((2048, 128), BF16),
            pltpu.VMEM((128, 2048), BF16),
            pltpu.VMEM((2, HALF, 256), F32),
            pltpu.VMEM((2048, 4096), BF16),
            pltpu.VMEM((2048, 4096), BF16),
            pltpu.VMEM((NQ, 128, 512), F32),
            pltpu.VMEM((NQ, 128, 512), BF16),
            pltpu.VMEM((NQ, 128, 512), BF16),
            pltpu.VMEM((NQ, 2, 512), F32),
            pltpu.VMEM((NQ, 2, 512), F32),
            pltpu.VMEM((NQ, NQ, 2, 512), F32),
            pltpu.VMEM((128, 128), F32),
            pltpu.VMEM((4096, 128), BF16),
            pltpu.VMEM((4096, 128), BF16),
            pltpu.VMEM((NK, 2, 128, 128), BF16),
            pltpu.VMEM((NK, 2, 128, 128), BF16),
            pltpu.VMEM((6, 2, 128, 128), BF16),
            dma((5,)),
            dma((NQ, 2)),
            dma((NQ, 2)),
            dma((NQ,)),
            dma((NQ,)),
            dma((NK, 2)),
            dma((NK, 2)),
            dma((NQ,)),
            dma((NQ,)),
            dma((NQ, len(STAT_BATCHES))),
            dma((NQ, len(STAT_BATCHES))),
            dma((NK,)),
            dma((NK,)),
            dma((6, 2)),
            dma((6, 2)),
        ],
        compiler_params=pltpu.CompilerParams(
            collective_id=0, has_side_effects=True, vmem_limit_bytes=60 * 1024 * 1024
        ),
        name="attention_backward",
    )(block_order, queries, keys, values, outputs, grad_out)


def solution(mesh):
    rows = P(("row", "col"), None)
    return jax.shard_map(
        per_device,
        mesh=mesh,
        in_specs=(rows, rows, rows, rows, rows, P()),
        out_specs=(rows, rows, rows),
        check_vma=False,
    )
```

```python
import functools
import math

import jax
import jax.numpy as jnp
from jax import lax
from jax.experimental import pallas as pl
from jax.experimental.pallas import tpu as pltpu
from jax.sharding import PartitionSpec as P

MESH = pl.DeviceIdType.MESH
F32 = jnp.float32
BF16 = jnp.bfloat16
HIDDEN = -1e30

NQ = 8
NK = 16
KEY_STEPS = (
    ((0, 0), (1, 0), (3, 0), (0, 1), (0, 3), (1, 1), (3, 3), (1, 3))
    + ((2, 1), (2, 3), (1, 2), (3, 2), (2, 0), (0, 2), (2, 2), (3, 1))
)
NEAR = (1, 2, 3, 4, 5, 6, 7, 15)
FAR = (12, 13, 8, 9, 10, 11)
CORNER = 14
HALF = 1024
STAT_BATCHES = ((6, 2), (0, 2), (2, 4))


def here():
    row = lax.axis_index("row")
    col = lax.axis_index("col")
    z = (row // 8) * 2 + col // 4
    return (row // 2) % 4, col % 4, z, row % 2


def device(x, y, z, core):
    return (((z // 2) * 4 + x) * 2 + core, (z % 2) * 4 + y)


def y_step(t):
    u = t // 2
    return u + (u // 2) * (5 - 2 * u)


def query_owner(t):
    x, y, z, core = here()
    return x, (y + 4 - y_step(t)) % 4, z, (core + t % 2) % 2


def query_reader(t):
    x, y, z, core = here()
    return x, (y + y_step(t)) % 4, z, (core + t % 2) % 2


def key_owner(j):
    x, y, z, core = here()
    dx, dz = KEY_STEPS[j]
    return (x + 4 - dx) % 4, y, (z + 4 - dz) % 4, core


def key_reader(j):
    x, y, z, core = here()
    dx, dz = KEY_STEPS[j]
    return (x + dx) % 4, y, (z + dz) % 4, core


def key_step(j, part):
    size = 1 if part == 0 else 3
    dx, dz = KEY_STEPS[j]
    return (size, 0) if dx == 2 else (0, size)


def halfway(j, part):
    step = key_step(j, part)
    dx, dz = KEY_STEPS[j]
    return KEY_STEPS.index(((dx - step[0]) % 4, (dz - step[1]) % 4))


def neighbour(step, sign):
    x, y, z, core = here()
    return (x + 4 + sign * step[0]) % 4, y, (z + 4 + sign * step[1]) % 4, core


def static_y(t):
    return (0, 1, 3, 2)[t // 2]


def seen_as(sender, t):
    dy = (static_y(t) - static_y(sender)) % 4
    return 2 * (0, 1, 3, 2)[dy] + (sender + t) % 2


def slot_of(place):
    row, col = device(*place)
    return row * 8 + col


def kernel(
    order,
    q_in,
    k_in,
    v_in,
    o_in,
    g_in,
    dq_out,
    dk_out,
    dv_out,
    qs,
    gs,
    own_o,
    delta,
    ks,
    vs,
    kt,
    scores,
    probs,
    dscores,
    u_sum,
    u_mine,
    u_got,
    stat_first,
    stat,
    stat_got,
    columns,
    qc,
    gc,
    part,
    part_got,
    relayed,
    local_sem,
    q_send,
    q_recv,
    d_send,
    d_recv,
    k_send,
    k_recv,
    u_send,
    u_recv,
    s_send,
    s_recv,
    p_send,
    p_recv,
    r_send,
    r_recv,
):
    dh = 128
    blk = 128
    heads = 4
    factor = 1.0 / math.sqrt(dh)
    scale2 = factor * math.log2(math.e)

    def remote(src, dst, send, recv, place):
        return pltpu.make_async_remote_copy(
            src_ref=src,
            dst_ref=dst,
            send_sem=send,
            recv_sem=recv,
            device_id=device(*place),
            device_id_type=MESH,
        )

    def q_copy(src_q, src_g, t, place):
        return (
            remote(src_q, qs.at[t], q_send.at[t, 0], q_recv.at[t, 0], place),
            remote(src_g, gs.at[t], q_send.at[t, 1], q_recv.at[t, 1], place),
        )

    def k_copy(j):
        rows = pl.ds(j * blk, blk)
        return (
            remote(k_in, ks.at[rows], k_send.at[j, 0], k_recv.at[j, 0], key_reader(j)),
            remote(v_in, vs.at[rows], k_send.at[j, 1], k_recv.at[j, 1], key_reader(j)),
        )

    def relay_keys(j, part):
        ref = (ks, vs)[part]
        return remote(
            ref.at[pl.ds(halfway(j, part) * blk, blk)],
            ref.at[pl.ds(j * blk, blk)],
            k_send.at[j, part],
            k_recv.at[j, part],
            neighbour(key_step(j, part), 1),
        )

    def relay_grads(j, part_):
        return remote(
            part.at[j, part_],
            relayed.at[j - 8, part_],
            r_send.at[j - 8, part_],
            r_recv.at[j - 8, part_],
            neighbour(key_step(j, part_), -1),
        )

    def d_copy(t):
        return remote(delta.at[0], delta.at[t], d_send.at[t], d_recv.at[t], query_reader(t))

    def u_copy(t):
        return remote(u_mine.at[t], u_got.at[t], u_send.at[t], u_recv.at[t], query_owner(t))

    def s_copy(t, batch):
        some = pl.ds(*STAT_BATCHES[batch])
        return remote(
            stat.at[some],
            stat_got.at[t, some],
            s_send.at[t, batch],
            s_recv.at[t, batch],
            query_owner(t),
        )

    def p_copy(j):
        return remote(part.at[j], part_got.at[j], p_send.at[j], p_recv.at[j], key_owner(j))

    barrier = pltpu.get_barrier_semaphore()
    for t in range(1, NQ):
        pl.semaphore_signal(barrier, inc=1, device_id=device(*query_reader(t)), device_id_type=MESH)
    for j in NEAR + (CORNER,):
        pl.semaphore_signal(barrier, inc=1, device_id=device(*key_reader(j)), device_id_type=MESH)
    locals_ = [
        pltpu.make_async_copy(o_in, own_o, local_sem.at[0]),
        pltpu.make_async_copy(g_in, gs.at[0], local_sem.at[1]),
        pltpu.make_async_copy(q_in, qs.at[0], local_sem.at[2]),
        pltpu.make_async_copy(k_in, ks.at[pl.ds(0, blk)], local_sem.at[3]),
        pltpu.make_async_copy(v_in, vs.at[pl.ds(0, blk)], local_sem.at[4]),
    ]
    for copy in locals_:
        copy.start()
    for copy in locals_:
        copy.wait()
    product = gs[0].astype(F32) * own_o[...].astype(F32)
    for h in range(heads):
        summed = jnp.sum(product[:, h * dh : (h + 1) * dh], axis=1, keepdims=True)
        wide = jnp.broadcast_to(summed, (blk, dh))
        delta[0, :, h * blk : (h + 1) * blk] = jnp.transpose(wide)[0:1, :]
    pl.semaphore_wait(barrier, NQ - 1 + len(NEAR) + 1)

    def start_keys(slots):
        copies = [k_copy(j) for j in slots]
        for part_ in range(2):
            for pair in copies:
                pair[part_].start()

    start_keys(NEAR)
    for t in (1, 2, 4):
        for copy in q_copy(q_in, g_in, t, query_reader(t)):
            copy.start()
    for t in range(1, NQ):
        d_copy(t).start()
    for copy in q_copy(q_in, g_in, 6, query_reader(6)):
        copy.start()

    def turn_keys(slots):
        for j in slots:
            kt[:, j * blk : (j + 1) * blk] = jnp.transpose(
                ks[j * blk : (j + 1) * blk, :].astype(F32)
            ).astype(BF16)

    x, y, z, core = here()
    row_less_col = lax.broadcasted_iota(jnp.int32, (blk, 2 * blk), 0) - (
        lax.broadcasted_iota(jnp.int32, (blk, 2 * blk), 1) % blk
    )
    chunk = 512
    per_chunk = chunk // blk

    def unit(t, half, with_u):
        q_order = order[slot_of(query_owner(t))]
        slots = range(half * 8, half * 8 + 8)
        penalty = {}
        for j in slots[1 - half :]:
            k_order = order[slot_of(key_owner(j))]
            penalty[j] = jnp.where(k_order < q_order, 0.0, -HIDDEN).astype(F32)

        def two_heads(ref, pair):
            return jnp.concatenate(
                [ref[t, :, (2 * pair + i) * dh : (2 * pair + i + 1) * dh] for i in range(2)], axis=0
            )

        def score_part(pair, q2, first, top8):
            rows = slice(first * blk, (first + per_chunk) * blk)
            s = lax.dot_general(
                ks[rows, :], q2, (((1,), (1,)), ((), ())), preferred_element_type=F32
            )
            for i in range(per_chunk):
                j = first + i
                n = j - half * 8
                tile = s[i * blk : (i + 1) * blk]
                if j == 0:
                    k_order = order[slot_of(key_owner(0))]
                    tile = jnp.where(row_less_col <= blk * (q_order - k_order), tile, HIDDEN)
                scores[pair, n * blk : (n + 1) * blk, :] = tile
                largest = jnp.max(tile.reshape(blk // 8, 8, 256), axis=0)
                top8 = jnp.maximum(top8, largest - penalty[j] if j > 0 else largest)
            return top8

        def grad_part(pair, g2, first, top, away, total8):
            lanes = pl.ds(pl.multiple_of(t * 512 + pair * 256, 256), 256)
            rows = slice(first * blk, (first + per_chunk) * blk)
            dp = lax.dot_general(
                vs[rows, :], g2, (((1,), (1,)), ((), ())), preferred_element_type=F32
            )
            for i in range(per_chunk):
                j = first + i
                n = j - half * 8
                tile_rows = slice(j * blk, (j + 1) * blk)
                shift = top + penalty[j] if j > 0 else top
                p = jnp.exp2(scores[pair, n * blk : (n + 1) * blk, :] * scale2 - shift)
                total8 += jnp.sum(p.reshape(blk // 8, 8, 256), axis=0)
                ds = p * (dp[i * blk : (i + 1) * blk] - away)
                probs[tile_rows, lanes] = p.astype(BF16)
                dscores[tile_rows, lanes] = ds.astype(BF16)
            return total8

        queries = [two_heads(qs, pair) for pair in range(2)]
        top8 = [jnp.full((8, 256), HIDDEN, F32) for pair in range(2)]
        for first in slots[::per_chunk]:
            top8[0] = score_part(0, queries[0], first, top8[0])
        for pair in range(2):
            own = slice(pair * 256, pair * 256 + 256)
            top = jnp.max(top8[pair], axis=0, keepdims=True) * scale2
            if half == 1:
                before = stat_first[t, 0:1, own]
                top = jnp.maximum(top, before)
            total8 = jnp.zeros((8, 256), F32)
            g2 = two_heads(gs, pair)
            away = delta[t, :, own]
            for first in slots[::per_chunk]:
                if pair == 0:
                    top8[1] = score_part(1, queries[1], first, top8[1])
                total8 = grad_part(pair, g2, first, top, away, total8)
            total = jnp.sum(total8, axis=0, keepdims=True)
            if with_u:
                lanes = pl.ds(pl.multiple_of(t * 512 + pair * 256, 256), 256)
                keys_ = slice(half * HALF, (half + 1) * HALF)
                du = jnp.dot(kt[:, keys_], dscores[keys_, lanes], preferred_element_type=F32)
            if half == 0:
                stat_first[t, 0:1, own] = top
                stat_first[t, 1:2, own] = total
                u_sum[t, :, own] = du
            else:
                shrink = jnp.exp2(before - top)
                stat[t, 0:1, own] = top
                stat[t, 1:2, own] = total + stat_first[t, 1:2, own] * shrink
                if with_u:
                    u_mine[t, :, own] = (du + u_sum[t, :, own] * shrink).astype(BF16)

    def first_half(t, carry):
        @pl.when(t > 0)
        def _():
            for copy in q_copy(q_in, g_in, t, query_reader(t)):
                copy.wait_recv()
            d_copy(t).wait_recv()

        @pl.when(jnp.logical_and(t > 1, t % 2 == 0))
        def _():
            for copy in q_copy(qs.at[t], gs.at[t], t + 1, (x, y, z, (core + 1) % 2)):
                copy.start()

        unit(t, 0, True)
        return carry

    def second_half(i, carry):
        t = (i + 6) % NQ
        unit(t, 1, True)

        @pl.when(t > 0)
        def _():
            u_copy(t).start()

        return carry

    def second_half_late(t, carry):
        unit(t, 1, False)
        return carry

    def late_u(t, carry):
        lanes = pl.ds(pl.multiple_of(t * 512, 512), 512)
        du = jnp.dot(kt[:, HALF:], dscores[HALF:, lanes], preferred_element_type=F32)
        shrink = jnp.exp2(stat_first[t, 0:1, :] - stat[t, 0:1, :])
        u_mine[t] = (du + u_sum[t] * shrink).astype(BF16)
        u_copy(t).start()
        return carry

    for j in NEAR:
        for part_, copy in enumerate(k_copy(j)):
            copy.wait_recv()
            for far in FAR:
                if halfway(far, part_) == j:
                    relay_keys(far, part_).start()
    start_keys((CORNER,))
    turn_keys(range(8))
    lax.fori_loop(0, NQ, first_half, 0)
    for j in FAR + (CORNER,):
        for copy in k_copy(j):
            copy.wait_recv()
    turn_keys(range(8, NK))
    lax.fori_loop(0, 4, second_half, 0)
    for t in range(1, NQ):
        s_copy(t, 0).start()
        s_copy(t, 1).start()
    lax.fori_loop(2, 6, second_half_late, 0)
    for t in range(1, NQ):
        s_copy(t, 2).start()
    lax.fori_loop(2, 6, late_u, 0)

    for t in range(1, NQ):
        for batch in range(len(STAT_BATCHES)):
            s_copy(t, batch).wait_recv()
    found = {n: [] for n in range(NQ)}
    for sender in range(NQ):
        for t in range(NQ):
            from_ = stat[t] if sender == 0 else stat_got[sender, t]
            found[seen_as(sender, t)].append((from_[0:1], from_[1:2]))
    log_totals = []
    for n in range(NQ):
        best = functools.reduce(jnp.maximum, [top for top, _ in found[n]])
        total = sum(part_total * jnp.exp2(top - best) for top, part_total in found[n])
        log_totals.append(best + jnp.log2(total))
    lines = []
    for source in (stat_first, stat):
        for t in range(NQ):
            line = jnp.exp2(source[t, 0:1, :] - log_totals[t])
            for h in range(heads):
                lines.append(line[:, h * blk : (h + 1) * blk])
    lines.append(jnp.zeros((blk - 2 * NQ * heads, blk), F32))
    columns[...] = jnp.transpose(jnp.concatenate(lines, axis=0))
    weights = []
    for sender in range(NQ):
        t = [n for n in range(NQ) if seen_as(sender, n) == 0][0]
        top = stat[t, 0:1, :] if sender == 0 else stat_got[sender, t, 0:1, :]
        weights.append(jnp.exp2(top - log_totals[0]) * factor)

    def scaled_rows(half):
        for t in range(NQ):
            for h in range(heads):
                n = t * heads + h
                c = columns[:, half * NQ * heads + n : half * NQ * heads + n + 1]
                place = slice(n * blk, (n + 1) * blk)
                lanes = slice(h * dh, (h + 1) * dh)
                qc[place, :] = (qs[t, :, lanes].astype(F32) * c).astype(BF16)
                gc[place, :] = (gs[t, :, lanes].astype(F32) * c).astype(BF16)

    def key_grads(first, count):
        rows = slice(first * blk, (first + count) * blk)
        dv = jnp.dot(probs[rows, :], gc[...], preferred_element_type=F32)
        dk = jnp.dot(dscores[rows, :], qc[...], preferred_element_type=F32) * factor
        for n in range(count):
            j = first + n
            part[j, 0] = dk[n * blk : (n + 1) * blk].astype(BF16)
            part[j, 1] = dv[n * blk : (n + 1) * blk].astype(BF16)

    def send_near(slots):
        for j in slots:
            for part_ in range(2):
                total = part[j, part_].astype(F32)
                extra = [far for far in FAR if halfway(far, part_) == j]
                for far in extra:
                    relay_grads(far, part_).wait_recv()
                    total += relayed[far - 8, part_].astype(F32)
                if extra:
                    part[j, part_] = total.astype(BF16)
            p_copy(j).start()

    scaled_rows(1)
    key_grads(8, 4)
    for j in (8, 9, 10, 11):
        for part_ in range(2):
            relay_grads(j, part_).start()
    key_grads(12, 4)
    for j in (12, 13):
        for part_ in range(2):
            relay_grads(j, part_).start()
    p_copy(CORNER).start()
    scaled_rows(0)
    key_grads(4, 4)
    send_near((5, 6, 7, 15, 4))
    key_grads(1, 3)
    send_near((1, 2, 3))
    key_grads(0, 1)

    for t in range(1, NQ):
        u_copy(t).wait_recv()
    for h in range(heads):
        lanes = slice(h * blk, (h + 1) * blk)
        acc = weights[0][:, lanes] * u_mine[0, :, lanes].astype(F32)
        for t in range(1, NQ):
            acc += weights[t][:, lanes] * u_got[t, :, lanes].astype(F32)
        dq_out[:, h * dh : (h + 1) * dh] = jnp.transpose(acc).astype(BF16)

    dk_sum = part[0, 0].astype(F32)
    dv_sum = part[0, 1].astype(F32)
    for j in (CORNER, 5, 6, 7, 15, 1, 2, 3, 4):
        p_copy(j).wait_recv()
        dk_sum += part_got[j, 0].astype(F32)
        dv_sum += part_got[j, 1].astype(F32)
    dk_out[...] = dk_sum.astype(BF16)
    dv_out[...] = dv_sum.astype(BF16)

    for j in NEAR + (CORNER,):
        for copy in k_copy(j):
            copy.wait_send()
        p_copy(j).wait_send()
    for j in FAR:
        for part_ in range(2):
            relay_keys(j, part_).wait_send()
            relay_grads(j, part_).wait_send()
    for t in range(1, NQ):
        for copy in q_copy(q_in, g_in, t, query_reader(t)):
            copy.wait_send()
        d_copy(t).wait_send()
        u_copy(t).wait_send()
        for batch in range(len(STAT_BATCHES)):
            s_copy(t, batch).wait_send()


def per_device(queries, keys, values, outputs, grad_out, block_order):
    anywhere = pl.BlockSpec(memory_space=pl.ANY)
    whole = pl.BlockSpec(memory_space=pltpu.VMEM)
    dma = pltpu.SemaphoreType.DMA
    return pl.pallas_call(
        kernel,
        out_shape=(
            jax.ShapeDtypeStruct((128, 512), BF16),
            jax.ShapeDtypeStruct((128, 128), BF16),
            jax.ShapeDtypeStruct((128, 128), BF16),
        ),
        in_specs=[pl.BlockSpec(memory_space=pltpu.SMEM)] + [anywhere] * 5,
        out_specs=(whole, whole, whole),
        scratch_shapes=[
            pltpu.VMEM((NQ, 128, 512), BF16),
            pltpu.VMEM((NQ, 128, 512), BF16),
            pltpu.VMEM((128, 512), BF16),
            pltpu.VMEM((NQ, 1, 512), F32),
            pltpu.VMEM((2048, 128), BF16),
            pltpu.VMEM((2048, 128), BF16),
            pltpu.VMEM((128, 2048), BF16),
            pltpu.VMEM((2, HALF, 256), F32),
            pltpu.VMEM((2048, 4096), BF16),
            pltpu.VMEM((2048, 4096), BF16),
            pltpu.VMEM((NQ, 128, 512), F32),
            pltpu.VMEM((NQ, 128, 512), BF16),
            pltpu.VMEM((NQ, 128, 512), BF16),
            pltpu.VMEM((NQ, 2, 512), F32),
            pltpu.VMEM((NQ, 2, 512), F32),
            pltpu.VMEM((NQ, NQ, 2, 512), F32),
            pltpu.VMEM((128, 128), F32),
            pltpu.VMEM((4096, 128), BF16),
            pltpu.VMEM((4096, 128), BF16),
            pltpu.VMEM((NK, 2, 128, 128), BF16),
            pltpu.VMEM((NK, 2, 128, 128), BF16),
            pltpu.VMEM((6, 2, 128, 128), BF16),
            dma((5,)),
            dma((NQ, 2)),
            dma((NQ, 2)),
            dma((NQ,)),
            dma((NQ,)),
            dma((NK, 2)),
            dma((NK, 2)),
            dma((NQ,)),
            dma((NQ,)),
            dma((NQ, len(STAT_BATCHES))),
            dma((NQ, len(STAT_BATCHES))),
            dma((NK,)),
            dma((NK,)),
            dma((6, 2)),
            dma((6, 2)),
        ],
        compiler_params=pltpu.CompilerParams(
            collective_id=0, has_side_effects=True, vmem_limit_bytes=60 * 1024 * 1024
        ),
        name="attention_backward",
    )(block_order, queries, keys, values, outputs, grad_out)


def solution(mesh):
    rows = P(("row", "col"), None)
    return jax.shard_map(
        per_device,
        mesh=mesh,
        in_specs=(rows, rows, rows, rows, rows, P()),
        out_specs=(rows, rows, rows),
        check_vma=False,
    )
```
